256 devices in a mesh: dp: 32 (over x, z_lo, core), tower: 8 (over z_hi, y).
Axes of the slice: x: 4, y: 4, z: 8 (z_hi: 2, z_lo: 4; z = z_hi * 4 + z_lo), core: 2. Of those that a mesh axis runs over, the one named last changes fastest.
Arguments:
- user_states: bfloat16 [12288, 1024], P('dp'), may hold values from -80 to 80
- head_gain: float32 [3, 1024], replicated, may hold values from 0.1 to 1.9
- item_table: bfloat16 [16384, 1024], P('tower'), may hold values from -5 to 5
- neg_ids: int32 [16384], P(('dp', 'tower')), may hold values from 0 to 16383, as said below
- pos_ids: int32 [12288], P('dp'), may hold values from 0 to 16383
- label_mask: int32 [3, 12288], P(None, 'dp'), may hold values 0 or 1
- seq_len: int32 [32], P('dp'), may hold values from 96 to 384
Outputs:
- pos_loss: float32 [3, 12288], P(None, 'dp')
- neg_grad: float32 [16384, 1024], P(('dp', 'tower'))
The draws below stay inside these ranges and needn't reach their ends.
Inputs may be any that keep to these rules, and one draw needn't show every extreme that they name: `neg_ids`: the 64 ids of block b (slots b * 64 onward) lie in rows t * 2048 to (t + 1) * 2048 - 1, with t = b % 8.
All inputs are finite; a program needn't handle non-finite values. No bound on the sum of `label_mask` on one device may be relied on, other than what follows from the above.
Results may differ from the reference program's by a relative error of at most 0.0037.
Values may be sent and summed in bfloat16 or wider, within the bound.
No kernel may reach another device: no remote copies, remote signals or barrier semaphores. Data moves between devices by JAX's collectives and lax.ppermute only.
A program may use at most 64 MiB of HBM per device.

```python
import math
import jax
import jax.numpy as jnp
from jax import lax

D = 1024
HEADS = 3
P_DEV = 384
NEG_DEV = 64
V_DEV = 2048
POSITIONS = 12288
NEG = 16384
VOCAB = 16384
N_DP = 32
N_TOWER = 8


def shared_table(key):
    return jnp.clip(jax.random.normal(key, (VOCAB, D), jnp.float32), -5.0, 5.0)


def shared_negatives(key):
    key = jax.random.fold_in(key, 11)
    blocks = jnp.arange(NEG, dtype=jnp.int32) // NEG_DEV
    owner = blocks % N_TOWER
    return (owner * V_DEV + jax.random.randint(key, (NEG,), 0, V_DEV)).astype(jnp.int32)


def draw_item_table(key, part):
    table = shared_table(key)
    return table.astype(jnp.bfloat16)


def draw_neg_ids(key, part):
    return shared_negatives(key)


def draw_user_states(key, part):
    key = jax.random.fold_in(key, 5)
    key_base = jax.random.fold_in(key, 0)
    base = jnp.clip(jax.random.normal(key_base, (POSITIONS, D), jnp.float32), -6.0, 6.0)
    return base.astype(jnp.bfloat16)


def draw_seq_len(key, part):
    key = jax.random.fold_in(key, 7)
    lengths = jax.random.randint(key, (N_DP,), P_DEV // 4, P_DEV + 1)
    return lengths.at[0].set(P_DEV).astype(jnp.int32)


def touch_ends(drawn, stream_key, least, top_value):
    extent = drawn.shape
    place = [jax.random.randint(jax.random.fold_in(stream_key, axis), (), 0, extent[axis]) for axis in range(len(extent))]
    drawn = drawn.at[tuple(place)].set(least)
    longest = extent.index(max(extent))
    place[longest] = (place[longest] + 1) % extent[longest]
    return drawn.at[tuple(place)].set(top_value)


def setup_inputs(seed: int = 0) -> dict:
    splits = jax.random.split(jax.random.key(seed), 8)
    user_states = draw_user_states(jax.random.fold_in(splits[7], 71), 0)
    head_gain = jnp.clip(1.0 + 0.18 * jax.random.normal(splits[1], (HEADS, D), jnp.float32), 0.1, 1.9)
    item_table = draw_item_table(jax.random.fold_in(splits[7], 71), 0)
    neg_ids = draw_neg_ids(jax.random.fold_in(splits[7], 71), 0)
    pos_ids = touch_ends(jax.random.randint(splits[4], (POSITIONS,), 0, VOCAB), jax.random.fold_in(splits[4], 1), 0, VOCAB - 1).astype(jnp.int32)
    label_mask = touch_ends((jax.random.randint(splits[5], (HEADS, POSITIONS), 0, 2) < 1).astype(jnp.int32), jax.random.fold_in(splits[5], 1), 0, 1)
    seq_len = draw_seq_len(jax.random.fold_in(splits[7], 71), 0)
    return {"user_states": user_states, "head_gain": head_gain, "item_table": item_table, "neg_ids": neg_ids, "pos_ids": pos_ids, "label_mask": label_mask, "seq_len": seq_len}


def reference(user_states, head_gain, item_table, neg_ids, pos_ids, label_mask, seq_len):
    inv = 1.0 / math.sqrt(D)
    emb = item_table[neg_ids]
    query = (user_states.astype(jnp.float32)[None] * head_gain[:, None, :]).astype(jnp.bfloat16)
    pos_emb = item_table[pos_ids]
    pos_score = lax.optimization_barrier(jnp.sum(query.astype(jnp.float32) * pos_emb.astype(jnp.float32)[None], -1)) * inv
    valid = (jnp.arange(P_DEV)[None, :] < seq_len[:, None]).reshape(POSITIONS)
    weight = label_mask.astype(jnp.float32) * valid.astype(jnp.float32)[None]
    blocks = query.reshape(HEADS, N_DP, P_DEV, D).transpose(1, 0, 2, 3).reshape(N_DP, HEADS * P_DEV, D)
    pos_blocks = pos_score.reshape(HEADS, N_DP, P_DEV).transpose(1, 0, 2).reshape(N_DP, HEADS * P_DEV)
    w_blocks = weight.reshape(HEADS, N_DP, P_DEV).transpose(1, 0, 2).reshape(N_DP, HEADS * P_DEV)

    def one_block(total, inputs):
        flat, pos_part, w_part = inputs
        scores = jnp.dot(flat, emb.T, preferred_element_type=jnp.float32) * inv
        top = jnp.maximum(lax.optimization_barrier(jnp.max(scores, axis=1)), pos_part)
        sums = lax.optimization_barrier(jnp.sum(jnp.exp(scores - top[:, None]), axis=1)) + jnp.exp(pos_part - top)
        lse = top + jnp.log(sums)
        prob = (w_part[:, None] * jnp.exp(scores - lse[:, None])).astype(jnp.bfloat16)
        total = total + jnp.dot(prob.T, flat, preferred_element_type=jnp.float32)
        return (total, lse)
    start = jnp.zeros((NEG, D), jnp.float32)
    total, lse_blocks = lax.scan(one_block, start, (blocks, pos_blocks, w_blocks))
    lse = lse_blocks.reshape(N_DP, HEADS, P_DEV).transpose(1, 0, 2).reshape(HEADS, POSITIONS)
    pos_loss = weight * (lse - pos_score)
    neg_grad = total * (NEG / math.sqrt(POSITIONS))
    return (pos_loss, neg_grad)
```

```python
import functools
import math

import jax
import jax.numpy as jnp
from jax import lax
from jax.experimental import pallas as pl
from jax.experimental.pallas import tpu as pltpu
from jax.sharding import Mesh
from jax.sharding import PartitionSpec as P

F32 = jnp.float32
BF16 = jnp.bfloat16
DP = ("x", "z", "core")
TOWER = ("zh", "y")


def one_hot_rows(ids_row, width):
    n = ids_row.shape[1]
    parts = []
    for a in range(0, n, 128):
        wide = jnp.broadcast_to(ids_row[:, a : a + 128].astype(F32), (128, 128))
        column = wide.T.astype(jnp.int32)
        lane = lax.broadcasted_iota(jnp.int32, (128, 128), 1)
        parts.append(
            jnp.concatenate(
                [(column == lane + v).astype(F32).astype(BF16) for v in range(0, width, 128)], axis=1
            )
        )
    return parts[0] if len(parts) == 1 else jnp.concatenate(parts, axis=0)


def score_kernel(
    inv, ids_ref, pos_ref, gain_ref, own_ref, other_ref, table_ref,
    e_ref, q_ref, m_ref, msg_ref, emb_ref, pos_emb_ref, msg_row,
):
    head = pl.program_id(0)
    rows = own_ref.shape[0]
    negs = emb_ref.shape[0]
    width = table_ref.shape[0]

    @pl.when(head == 0)
    def _():
        for a in range(0, negs, 128):
            hot = one_hot_rows(ids_ref[a // 128 : a // 128 + 1, :], width)
            emb_ref[a : a + 128, :] = jnp.dot(hot, table_ref[...], preferred_element_type=F32).astype(BF16)
        for a in range(0, rows, 128):
            hot = one_hot_rows(pos_ref[a // 128 : a // 128 + 1, :], width)
            pos_emb_ref[a : a + 128, :] = jnp.dot(hot, table_ref[...], preferred_element_type=F32).astype(BF16)

    gain = gain_ref[pl.ds(head, 1), :]
    q_ref[:rows, :] = (own_ref[...].astype(F32) * gain).astype(BF16)
    q_ref[rows:, :] = (other_ref[...].astype(F32) * gain).astype(BF16)
    nt = (((1,), (1,)), ((), ()))
    block = 256
    for a in range(0, 2 * rows, block):
        s = lax.dot_general(emb_ref[...], q_ref[a : a + block, :], nt, preferred_element_type=F32) * inv
        m = jnp.max(s, axis=0, keepdims=True)
        e = jnp.exp(s - m)
        e_ref[:, a : a + block] = e
        m_ref[pl.ds(head, 1), a : a + block] = m
        msg_row[:, a : a + block] = m + jnp.log(jnp.sum(e, axis=0, keepdims=True))
    pos = []
    owned = []
    for a in range(0, rows, 128):
        d = lax.dot_general(pos_emb_ref[a : a + 128, :], q_ref[a : a + 128, :], nt, preferred_element_type=F32)
        diag = lax.broadcasted_iota(jnp.int32, d.shape, 0) == lax.broadcasted_iota(jnp.int32, d.shape, 1)
        pos.append(jnp.sum(jnp.where(diag, d, 0.0), axis=0, keepdims=True) * inv)
        ids = pos_ref[a // 128 : a // 128 + 1, :]
        owned.append((ids >= 0) & (ids < width))
    for i, a in enumerate(range(0, rows, 128)):
        base = msg_row[:, a : a + 128]
        top = jnp.maximum(base, pos[i])
        both = top + jnp.log(jnp.exp(base - top) + jnp.exp(pos[i] - top))
        msg_row[:, a : a + 128] = jnp.where(owned[i], both, base)
        msg_row[:, 2 * rows + a : 2 * rows + a + 128] = pos[i]
    for k in range(msg_ref.shape[0]):
        msg_ref[k, pl.ds(head, 1), :] = msg_row[...]


def scores(inv, ids, pos, gain, own, other, table, group):
    rows, width = own.shape
    heads = gain.shape[0]
    negs = ids.size
    full = lambda *shape: pl.BlockSpec(shape, lambda h: (0,) * len(shape))
    return pl.pallas_call(
        functools.partial(score_kernel, inv),
        grid=(heads,),
        in_specs=[
            full(*ids.shape), full(*pos.shape), full(*gain.shape),
            full(rows, width), full(rows, width), full(*table.shape),
        ],
        out_specs=[
            pl.BlockSpec((negs, 2 * rows), lambda h: (0, h)),
            pl.BlockSpec((None, 2 * rows, width), lambda h: (h, 0, 0)),
            full(heads, 2 * rows),
            full(group, heads, 3 * rows),
        ],
        out_shape=[
            jax.ShapeDtypeStruct((negs, heads * 2 * rows), F32),
            jax.ShapeDtypeStruct((heads, 2 * rows, width), BF16),
            jax.ShapeDtypeStruct((heads, 2 * rows), F32),
            jax.ShapeDtypeStruct((group, heads, 3 * rows), F32),
        ],
        scratch_shapes=[
            pltpu.VMEM((negs, width), BF16),
            pltpu.VMEM((rows, width), BF16),
            pltpu.VMEM((1, 3 * rows), F32),
        ],
        compiler_params=pltpu.CompilerParams(vmem_limit_bytes=48 * 2**20),
    )(ids, pos, gain, own, other, table)


def combine_kernel(core_ref, msg_ref, m_ref, w_ref, w_other_ref, c_ref, loss_ref):
    rows = w_ref.shape[1]
    half = msg_ref.shape[0] // 2
    core = core_ref[0]
    same = [msg_ref[core * half + k] for k in range(half)]
    cross = [msg_ref[(1 - core) * half + k] for k in range(half)]
    own = [r[:, :rows] for r in same] + [r[:, rows : 2 * rows] for r in cross]
    other = [r[:, rows : 2 * rows] for r in same] + [r[:, :rows] for r in cross]

    def fold(parts):
        top = functools.reduce(jnp.maximum, parts)
        return top + jnp.log(sum(jnp.exp(r - top) for r in parts))

    lse, lse_other = fold(own), fold(other)
    pos = sum(r[:, 2 * rows :] for r in same)
    loss_ref[...] = w_ref[...] * (lse - pos)
    c_ref[:, :rows] = w_ref[...] * jnp.exp(m_ref[:, :rows] - lse)
    c_ref[:, rows:] = w_other_ref[...] * jnp.exp(m_ref[:, rows:] - lse_other)


def combine(core, msg, m, w, w_other):
    vm = pl.BlockSpec(memory_space=pltpu.VMEM)
    return pl.pallas_call(
        combine_kernel,
        in_specs=[pl.BlockSpec(memory_space=pltpu.SMEM), vm, vm, vm, vm],
        out_specs=[vm, vm],
        out_shape=[jax.ShapeDtypeStruct(m.shape, F32), jax.ShapeDtypeStruct(w.shape, F32)],
    )(core, msg, m, w, w_other)


def grad_kernel(c_ref, e_ref, q_ref, out_ref, acc_ref):
    head = pl.program_id(0)
    p = (e_ref[...] * c_ref[pl.ds(head, 1), :]).astype(BF16)
    part = jnp.dot(p, q_ref[...], preferred_element_type=F32)

    @pl.when(head == 0)
    def _():
        acc_ref[...] = part

    @pl.when(head > 0)
    def _():
        acc_ref[...] += part

    @pl.when(head == pl.num_programs(0) - 1)
    def _():
        out_ref[...] = acc_ref[...].astype(out_ref.dtype)


def grad(c, e, q, piece, pieces, dtype):
    heads, rows, width = q.shape
    size = e.shape[0] // pieces
    return pl.pallas_call(
        grad_kernel,
        grid=(heads,),
        in_specs=[
            pl.BlockSpec((heads, rows), lambda h: (0, 0)),
            pl.BlockSpec((size, rows), lambda h: (piece, h)),
            pl.BlockSpec((None, rows, width), lambda h: (h, 0, 0)),
        ],
        out_specs=pl.BlockSpec((size, width), lambda h: (0, 0)),
        out_shape=jax.ShapeDtypeStruct((size, width), dtype),
        scratch_shapes=[pltpu.VMEM((size, width), F32)],
        compiler_params=pltpu.CompilerParams(vmem_limit_bytes=32 * 2**20),
        cost_estimate=pl.CostEstimate(
            flops=2 * size * heads * rows * width,
            bytes_accessed=4 * size * heads * rows + 2 * q.size,
            transcendentals=0,
        ),
    )(c, e, q)


def shards(nx, nz, user_states, head_gain, item_table, neg_ids, pos_ids, label_mask, seq_len):
    rows, width = user_states.shape
    heads = head_gain.shape[0]
    table_rows = item_table.shape[0]
    neg_dev = neg_ids.shape[0]
    group = lax.axis_size("core") * lax.axis_size("zh") * lax.axis_size("y")
    n_dev = nx * nz * group
    factor = (neg_dev * n_dev) / math.sqrt(rows * nx * nz * lax.axis_size("core"))
    x, z, core = lax.axis_index("x"), lax.axis_index("z"), lax.axis_index("core")
    offset = (lax.axis_index("zh") * lax.axis_size("y") + lax.axis_index("y")) * table_rows

    valid = (jnp.arange(rows) < seq_len[0]).astype(F32)
    w = label_mask.astype(F32) * valid[None]
    swap = [(0, 1), (1, 0)]
    other = lax.ppermute(user_states, "core", swap)
    w_other = lax.ppermute(w, "core", swap)

    slots = jnp.zeros((nx, nz, neg_dev), jnp.int32)
    slots = lax.dynamic_update_slice(slots, (neg_ids - offset)[None, None], (x, z, 0))
    slots = lax.psum(slots, ("x", "z"))
    slots = jnp.roll(slots, (-x, -z), (0, 1))
    ids = slots.reshape(-1, 128)
    pos = (pos_ids - offset).reshape(-1, 128)

    e, q, m, msg = scores(1.0 / math.sqrt(width), ids, pos, head_gain, user_states, other, item_table, group)
    msg = lax.all_to_all(msg, ("core",) + TOWER, 0, 0, tiled=True)
    c, pos_loss = combine(core.reshape(1), msg, m, w, w_other)

    def shifted(value, axis, size, by):
        return lax.ppermute(value, axis, [(i, (i + by) % size) for i in range(size)])

    order = [2, 1, 3]
    sent = [shifted(grad(c, e, q, k, nx, BF16), "x", nx, k) for k in order]
    total = grad(c, e, q, 0, nx, F32)
    for piece in sent:
        total = total + piece.astype(F32)
    parts = [total[k * neg_dev : (k + 1) * neg_dev] for k in range(nz)]
    sent = [shifted(parts[k].astype(BF16), "z", nz, k) for k in (2, 1, 3)]
    out = parts[0]
    for piece in sent:
        out = out + piece.astype(F32)
    return pos_loss, out * factor


def solution(mesh):
    nx, nz = 4, 4
    devices = mesh.devices.reshape(nx, nz, 2, 2, 4)
    wide = Mesh(devices, DP + TOWER)
    placed = (
        P(DP, None),
        P(),
        P(TOWER, None),
        P(DP + TOWER),
        P(DP),
        P(None, DP),
        P(DP),
    )
    return jax.shard_map(
        functools.partial(shards, nx, nz),
        mesh=wide,
        in_specs=placed,
        out_specs=(P(None, DP), P(DP + TOWER, None)),
        check_vma=False,
    )
```

```python
import functools
import math

import jax
import jax.numpy as jnp
from jax import lax
from jax.experimental import pallas as pl
from jax.experimental.pallas import tpu as pltpu
from jax.sharding import Mesh
from jax.sharding import PartitionSpec as P

F32 = jnp.float32
BF16 = jnp.bfloat16
DP = ("x", "z", "core")
TOWER = ("zh", "y")
LOG2E = math.log2(math.e)
NT = (((1,), (1,)), ((), ()))
ORDER = (2, 0, 1, 3)


def full(*shape):
    return pl.BlockSpec(shape, lambda *_: (0,) * len(shape))


def one_hot_rows(ids_row, width):
    column = jnp.broadcast_to(ids_row.astype(F32), (128, 128)).T
    lane = lax.broadcasted_iota(jnp.int32, (128, 128), 1).astype(F32)
    return jnp.concatenate(
        [jnp.where(column == lane + float(v), 1.0, 0.0).astype(BF16) for v in range(0, width, 128)], axis=1
    )


def score_kernel(inv, nx, nz, x_ref, z_ref, off_ref, ids_ref, pos_ref, gain_ref, own_ref, other_ref, table_hbm,
    e_ref, q_ref, m_ref, msg_ref, table_ref, emb_ref, pos_emb_ref, msg_row, sem):
    head = pl.program_id(0)
    rows = own_ref.shape[0]
    nd = ids_ref.shape[1]
    negs = emb_ref.shape[0]
    width = table_ref.shape[0]
    off = off_ref[0]
    @pl.when(head == 0)
    def _():
        copy = pltpu.make_async_copy(table_hbm, table_ref, sem)
        copy.start()
        copy.wait()
        x, z = x_ref[0], z_ref[0]
        for a in range(0, rows, 128):
            hot = one_hot_rows(pos_ref[:, a : a + 128] - off, width)
            pos_emb_ref[a : a + 128, :] = jnp.dot(hot, table_ref[...], preferred_element_type=F32).astype(BF16)
        for b in range(0, nx * nz, 2):
            pair = []
            for i in (b, b + 1):
                rx, rz = ORDER[i // nz], i % nz
                row = lax.rem(x + rx, nx) * nz + lax.rem(z + rz, nz)
                pair.append(ids_ref[pl.ds(row, 1), :] - off)
            hot = one_hot_rows(jnp.concatenate(pair, axis=1), width)
            emb_ref[b * nd : (b + 2) * nd, :] = jnp.dot(hot, table_ref[...], preferred_element_type=F32).astype(BF16)
    gain = gain_ref[pl.ds(head, 1), :]
    q_ref[:rows, :] = (own_ref[...].astype(F32) * gain).astype(BF16)
    q_ref[rows:, :] = (other_ref[...].astype(F32) * gain).astype(BF16)
    block = 256
    for a in range(0, 2 * rows, block):
        s = lax.dot_general(emb_ref[...], q_ref[a : a + block, :], NT, preferred_element_type=F32)
        m = jnp.max(s, axis=0, keepdims=True)
        e = jnp.exp2((s - m) * (inv * LOG2E))
        e_ref[:, a : a + block] = e
        m_ref[pl.ds(head, 1), a : a + block] = m * inv
        msg_row[:, a : a + block] = m * inv + jnp.log(jnp.sum(e, axis=0, keepdims=True))
    for a in range(0, rows, 128):
        d = lax.dot_general(pos_emb_ref[a : a + 128, :], q_ref[a : a + 128, :], NT, preferred_element_type=F32)
        diag = lax.broadcasted_iota(jnp.int32, d.shape, 0) == lax.broadcasted_iota(jnp.int32, d.shape, 1)
        pos = jnp.sum(jnp.where(diag, d, 0.0), axis=0, keepdims=True) * inv
        ids = pos_ref[:, a : a + 128] - off
        owned = (ids >= 0) & (ids < width)
        base = msg_row[:, a : a + 128]
        top = jnp.maximum(base, pos)
        both = top + jnp.log(jnp.exp(base - top) + jnp.exp(pos - top))
        msg_row[:, a : a + 128] = jnp.where(owned, both, base)
        msg_row[:, 2 * rows + a : 2 * rows + a + 128] = pos
    msg_ref[pl.ds(head, 1), :] = msg_row[...]

def scores(inv, nx, nz, x, z, off, ids, pos, gain, own, other, table):
    rows, width = own.shape
    heads = gain.shape[0]
    negs = ids.size
    sm = pl.BlockSpec(memory_space=pltpu.SMEM)
    return pl.pallas_call(
        functools.partial(score_kernel, inv, nx, nz),
        grid=(heads,),
        in_specs=[sm, sm, sm, full(*ids.shape), full(*pos.shape), full(*gain.shape),
            full(rows, width), full(rows, width), pl.BlockSpec(memory_space=pl.ANY)],
        out_specs=[
            pl.BlockSpec((negs, 2 * rows), lambda h: (0, h)),
            pl.BlockSpec((None, 2 * rows, width), lambda h: (h, 0, 0)),
            full(heads, 2 * rows),
            full(heads, 3 * rows),
        ],
        out_shape=[
            jax.ShapeDtypeStruct((negs, heads * 2 * rows), F32),
            jax.ShapeDtypeStruct((heads, 2 * rows, width), BF16),
            jax.ShapeDtypeStruct((heads, 2 * rows), F32),
            jax.ShapeDtypeStruct((heads, 3 * rows), F32),
        ],
        scratch_shapes=[
            pltpu.VMEM(table.shape, BF16),
            pltpu.VMEM((negs, width), BF16),
            pltpu.VMEM((rows, width), BF16),
            pltpu.VMEM((1, 3 * rows), F32),
            pltpu.SemaphoreType.DMA,
        ],
        compiler_params=pltpu.CompilerParams(vmem_limit_bytes=30 * 2**20),
    )(x, z, off, ids, pos, gain, own, other, table)


def pair_sum(a, b):
    top = jnp.maximum(a, b)
    return top + jnp.log(jnp.exp(a - top) + jnp.exp(b - top))


def fold_kernel(*refs):
    parts, out_ref = [r[...] for r in refs[:-1]], refs[-1]
    cut = out_ref.shape[1] // 3 * 2
    top = functools.reduce(jnp.maximum, [r[:, :cut] for r in parts])
    out_ref[:, :cut] = top + jnp.log(sum(jnp.exp(r[:, :cut] - top) for r in parts))
    out_ref[:, cut:] = sum(r[:, cut:] for r in parts)


def fold(*parts):
    shape = parts[0].shape
    return pl.pallas_call(
        fold_kernel,
        grid=(1,),
        in_specs=[full(*shape)] * len(parts),
        out_specs=full(*shape),
        out_shape=jax.ShapeDtypeStruct(shape, F32),
        compiler_params=pltpu.CompilerParams(vmem_limit_bytes=2**20),
    )(*parts)


def weights(part_ref, cross_ref, m_ref, w_ref, w_other_ref, c_ref, loss_ref):
    rows = w_ref.shape[1]
    lse = pair_sum(part_ref[:, :rows], cross_ref[:, rows : 2 * rows])
    lse_other = pair_sum(part_ref[:, rows : 2 * rows], cross_ref[:, :rows])
    loss_ref[...] = w_ref[...] * (lse - part_ref[:, 2 * rows :])
    c_ref[:, :rows] = w_ref[...] * jnp.exp(m_ref[:, :rows] - lse)
    c_ref[:, rows:] = w_other_ref[...] * jnp.exp(m_ref[:, rows:] - lse_other)


def products(c_ref, e_ref, q_ref, outs, p_ref):
    heads, rows = c_ref.shape
    for h in range(heads):
        part = slice(h * rows, (h + 1) * rows)
        p_ref[:, part] = (e_ref[:, part] * c_ref[h : h + 1, :]).astype(BF16)
    term = jnp.dot(p_ref[...], q_ref[...].reshape(heads * rows, -1), preferred_element_type=F32)
    at = 0
    for out in outs:
        n = out.shape[0]
        out[...] = term[at : at + n, :].astype(out.dtype)
        at += n


def first_kernel(part_ref, cross_ref, m_ref, w_ref, w_other_ref, e_ref, q_ref, c_ref, loss_ref, *rest):
    weights(part_ref, cross_ref, m_ref, w_ref, w_other_ref, c_ref, loss_ref)
    products(c_ref, e_ref, q_ref, rest[:-1], rest[-1])


def next_kernel(c_ref, e_ref, q_ref, *rest):
    products(c_ref, e_ref, q_ref, rest[:-1], rest[-1])


def grad(small, e, q, size, index, outs):
    heads, rows, width = q.shape
    first = len(small) > 1
    made = [(heads, rows), (heads, rows // 2)] if first else []
    shapes = [jax.ShapeDtypeStruct(s, F32) for s in made] + [jax.ShapeDtypeStruct((n, width), d) for n, d in outs]
    return pl.pallas_call(
        first_kernel if first else next_kernel,
        grid=(1,),
        in_specs=[full(*s.shape) for s in small]
        + [pl.BlockSpec((size, heads * rows), lambda _: (index, 0)), full(*q.shape)],
        out_specs=[full(*s.shape) for s in shapes],
        out_shape=shapes,
        scratch_shapes=[pltpu.VMEM((size, heads * rows), BF16)],
        compiler_params=pltpu.CompilerParams(vmem_limit_bytes=(10 + size // 32) * 2**20),
        cost_estimate=pl.CostEstimate(
            flops=2 * size * heads * rows * width,
            bytes_accessed=4 * size * heads * rows + 2 * q.size,
            transcendentals=0,
        ),
    )(*small, e, q)


def shards(nx, nz, user_states, head_gain, item_table, neg_ids, pos_ids, label_mask, seq_len):
    rows, width = user_states.shape
    heads = head_gain.shape[0]
    table_rows = item_table.shape[0]
    neg_dev = neg_ids.shape[0]
    n_dp = nx * nz * lax.axis_size("core")
    factor = neg_dev * n_dp * lax.axis_size("zh") * lax.axis_size("y") / math.sqrt(rows * n_dp)
    x, z = lax.axis_index("x"), lax.axis_index("z")
    offset = (lax.axis_index("zh") * lax.axis_size("y") + lax.axis_index("y")) * table_rows

    def shifted(value, axis, size, by):
        return lax.ppermute(value, axis, [(i, (i + by) % size) for i in range(size)])

    valid = (jnp.arange(rows) < seq_len[0]).astype(F32)
    w = label_mask.astype(F32) * valid[None]
    other = shifted(user_states, "core", 2, 1)
    w_other = shifted(w, "core", 2, 1)

    slot = lax.broadcasted_iota(jnp.int32, (nx * nz, neg_dev), 0)
    slots = lax.psum(jnp.where(slot == x * nz + z, neg_ids[None], 0), ("x", "z"))

    e, q, m, msg = scores(
        1.0 / math.sqrt(width), nx, nz, x.reshape(1), z.reshape(1), offset.reshape(1), slots, pos_ids[None],
        head_gain, user_states, other, item_table,
    )
    msg = fold(msg, *[lax.ppermute(msg, "y", [(i, i ^ k) for i in range(4)]) for k in (2, 1, 3)])
    part = fold(msg, shifted(msg, "zh", 2, 1))
    cross = shifted(part, "core", 2, 1)

    quarter = nz * neg_dev
    half = quarter // 2
    c, pos_loss, far_a, far_b = grad((part, cross, m, w, w_other), e, q, quarter, 0, [(half, BF16)] * 2)
    far_a, far_b = shifted(far_a, "x", nx, 1), shifted(far_b, "x", nx, -1)
    up_a, up_b, down_a, down_b = grad(
        (c,), e, q, 2 * quarter, 1, [(half, F32), (half, BF16), (half, BF16), (half, F32)]
    )
    up_b, down_a = shifted(up_b, "x", nx, 1), shifted(down_a, "x", nx, -1)
    own_a, own_b = grad((c,), e, q, quarter, 1, [(half, F32)] * 2)
    far_a, far_b = lax.optimization_barrier((far_a, far_b))
    up_a = shifted((up_a + far_a.astype(F32)).astype(BF16), "x", nx, 1)
    down_b = shifted((down_b + far_b.astype(F32)).astype(BF16), "x", nx, -1)
    own_a = own_a + down_a.astype(F32) + up_a.astype(F32)
    own_b = own_b + up_b.astype(F32) + down_b.astype(F32)
    total = jnp.concatenate([own_a, own_b], axis=0)

    parts = [total[k * neg_dev : (k + 1) * neg_dev] for k in range(nz)]
    sent = [shifted(parts[k].astype(BF16), "z", nz, k) for k in (2, 1, 3)]
    out = parts[0]
    for piece in sent:
        out = out + piece.astype(F32)
    return pos_loss, out * factor


def solution(mesh):
    nx, nz = 4, 4
    wide = Mesh(mesh.devices.reshape(nx, nz, 2, 2, 4), DP + TOWER)
    placed = (
        P(DP, None),
        P(),
        P(TOWER, None),
        P(DP + TOWER),
        P(DP),
        P(None, DP),
        P(DP),
    )
    return jax.shard_map(
        functools.partial(shards, nx, nz),
        mesh=wide,
        in_specs=placed,
        out_specs=(P(None, DP), P(DP + TOWER, None)),
        check_vma=False,
    )
```

```python
import functools
import math

import jax
import jax.numpy as jnp
from jax import lax
from jax.experimental import pallas as pl
from jax.experimental.pallas import tpu as pltpu
from jax.sharding import Mesh
from jax.sharding import PartitionSpec as P

F32 = jnp.float32
BF16 = jnp.bfloat16
DP = ("x", "z", "core")
TOWER = ("zh", "y")
LOG2E = math.log2(math.e)
NT = (((1,), (1,)), ((), ()))
ORDER = (2, 0, 1, 3)
Z_ORDER = (2, 3, 1, 0)


def full(*shape):
    return pl.BlockSpec(shape, lambda *_: (0,) * len(shape))


def one_hot_rows(ids_row, width):
    column = jnp.broadcast_to(ids_row.astype(F32), (128, 128)).T
    lane = lax.broadcasted_iota(jnp.int32, (128, 128), 1).astype(F32)
    return jnp.concatenate(
        [jnp.where(column == lane + float(v), 1.0, 0.0).astype(BF16) for v in range(0, width, 128)], axis=1
    )


def score_kernel(
    inv, nx, nz, x_ref, z_ref, off_ref, ids_ref, pos_ref, gain_ref, own_ref, other_ref, table_hbm,
    e_ref, q_ref, m_ref, msg_ref, table_ref, emb_ref, pos_emb_ref, sem,
):
    heads = gain_ref.shape[0]
    rows = own_ref.shape[0]
    nd = ids_ref.shape[1]
    width = table_ref.shape[0]
    off = off_ref[0]
    x, z = x_ref[0], z_ref[0]
    copy = pltpu.make_async_copy(table_hbm, table_ref, sem)
    copy.start()
    for head in range(heads):
        gain = gain_ref[head : head + 1, :]
        q_ref[head, :rows, :] = (own_ref[...].astype(F32) * gain).astype(BF16)
        q_ref[head, rows:, :] = (other_ref[...].astype(F32) * gain).astype(BF16)
    copy.wait()
    for b in range(0, nx * nz, 2):
        pair = []
        for i in (b, b + 1):
            rx, rz = ORDER[i // nz], Z_ORDER[i % nz]
            row = lax.rem(x + rx, nx) * nz + lax.rem(z + rz, nz)
            pair.append(ids_ref[pl.ds(row, 1), :] - off)
        hot = one_hot_rows(jnp.concatenate(pair, axis=1), width)
        emb_ref[b * nd : (b + 2) * nd, :] = jnp.dot(hot, table_ref[...], preferred_element_type=F32).astype(BF16)
    pos_ids = [pos_ref[a : a + 128].reshape(1, 128) - off for a in range(0, rows, 128)]
    for i, ids in enumerate(pos_ids):
        hot = one_hot_rows(ids, width)
        pos_emb_ref[i * 128 : i * 128 + 128, :] = jnp.dot(hot, table_ref[...], preferred_element_type=F32).astype(BF16)
    block = 256
    for head in range(heads):
        for a in range(0, 2 * rows, block):
            s = lax.dot_general(emb_ref[...], q_ref[head, a : a + block, :], NT, preferred_element_type=F32)
            m = jnp.max(s, axis=0, keepdims=True)
            e = jnp.exp2((s - m) * (inv * LOG2E))
            at = head * 2 * rows + a
            e_ref[:, at : at + block] = e
            m_ref[head : head + 1, a : a + block] = m * inv
            msg_ref[head : head + 1, a : a + block] = m * inv + jnp.log(jnp.sum(e, axis=0, keepdims=True))
        for i, ids in enumerate(pos_ids):
            a = i * 128
            d = lax.dot_general(
                pos_emb_ref[a : a + 128, :], q_ref[head, a : a + 128, :], NT, preferred_element_type=F32
            )
            diag = lax.broadcasted_iota(jnp.int32, d.shape, 0) == lax.broadcasted_iota(jnp.int32, d.shape, 1)
            pos = jnp.sum(jnp.where(diag, d, 0.0), axis=0, keepdims=True) * inv
            owned = (ids >= 0) & (ids < width)
            base = msg_ref[head : head + 1, a : a + 128]
            msg_ref[head : head + 1, a : a + 128] = jnp.where(owned, pair_sum(base, pos), base)
            msg_ref[head : head + 1, 2 * rows + a : 2 * rows + a + 128] = pos


def scores(inv, nx, nz, x, z, off, ids, pos, gain, own, other, table):
    rows, width = own.shape
    heads = gain.shape[0]
    negs = ids.size
    sm = pl.BlockSpec(memory_space=pltpu.SMEM)
    return pl.pallas_call(
        functools.partial(score_kernel, inv, nx, nz),
        grid=(1,),
        in_specs=[sm, sm, sm, full(*ids.shape), full(*pos.shape), full(*gain.shape),
            full(rows, width), full(rows, width), pl.BlockSpec(memory_space=pl.ANY)],
        out_specs=[
            full(negs, heads * 2 * rows),
            full(heads, 2 * rows, width),
            full(heads, 2 * rows),
            full(heads, 3 * rows),
        ],
        out_shape=[
            jax.ShapeDtypeStruct((negs, heads * 2 * rows), F32),
            jax.ShapeDtypeStruct((heads, 2 * rows, width), BF16),
            jax.ShapeDtypeStruct((heads, 2 * rows), F32),
            jax.ShapeDtypeStruct((heads, 3 * rows), F32),
        ],
        scratch_shapes=[
            pltpu.VMEM(table.shape, BF16),
            pltpu.VMEM((negs, width), BF16),
            pltpu.VMEM((rows, width), BF16),
            pltpu.SemaphoreType.DMA,
        ],
        compiler_params=pltpu.CompilerParams(vmem_limit_bytes=30 * 2**20),
    )(x, z, off, ids, pos, gain, own, other, table)


def pair_sum(a, b):
    top = jnp.maximum(a, b)
    return top + jnp.log(jnp.exp(a - top) + jnp.exp(b - top))


def fold_kernel(*refs):
    parts, out_ref = [r[...] for r in refs[:-1]], refs[-1]
    cut = out_ref.shape[1] // 3 * 2
    top = functools.reduce(jnp.maximum, [r[:, :cut] for r in parts])
    out_ref[:, :cut] = top + jnp.log(sum(jnp.exp(r[:, :cut] - top) for r in parts))
    out_ref[:, cut:] = sum(r[:, cut:] for r in parts)


def fold(*parts):
    shape = parts[0].shape
    return pl.pallas_call(
        fold_kernel,
        grid=(1,),
        in_specs=[full(*shape)] * len(parts),
        out_specs=full(*shape),
        out_shape=jax.ShapeDtypeStruct(shape, F32),
        compiler_params=pltpu.CompilerParams(vmem_limit_bytes=2**20),
    )(*parts)


def mask_kernel(len_ref, mask_ref, msg_ref, near_ref, out_ref):
    rows = mask_ref.shape[1]
    a, b = msg_ref[...], near_ref[...]
    out_ref[:, : 2 * rows] = pair_sum(a[:, : 2 * rows], b[:, : 2 * rows])
    out_ref[:, 2 * rows : 3 * rows] = a[:, 2 * rows :] + b[:, 2 * rows :]
    valid = lax.broadcasted_iota(jnp.int32, mask_ref.shape, 1) < len_ref[0]
    out_ref[:, 3 * rows :] = jnp.where(valid, mask_ref[...].astype(F32), 0.0)


def fold_with_mask(seq_len, mask, msg, near):
    heads, rows = mask.shape
    return pl.pallas_call(
        mask_kernel,
        grid=(1,),
        in_specs=[pl.BlockSpec(memory_space=pltpu.SMEM), full(*mask.shape), full(*msg.shape), full(*msg.shape)],
        out_specs=full(heads, 4 * rows),
        out_shape=jax.ShapeDtypeStruct((heads, 4 * rows), F32),
        compiler_params=pltpu.CompilerParams(vmem_limit_bytes=2**20),
    )(seq_len, mask, msg, near)


def weights(part_ref, cross_ref, m_ref, c_ref, loss_ref):
    rows = loss_ref.shape[1]
    w = part_ref[:, 3 * rows :]
    lse = pair_sum(part_ref[:, :rows], cross_ref[:, rows : 2 * rows])
    lse_other = pair_sum(part_ref[:, rows : 2 * rows], cross_ref[:, :rows])
    loss_ref[...] = w * (lse - part_ref[:, 2 * rows : 3 * rows])
    c_ref[:, :rows] = w * jnp.exp(m_ref[:, :rows] - lse)
    c_ref[:, rows:] = cross_ref[:, 3 * rows :] * jnp.exp(m_ref[:, rows:] - lse_other)


def products(c_ref, e_ref, q_ref, outs, p_ref):
    heads, rows = c_ref.shape
    for h in range(heads):
        part = slice(h * rows, (h + 1) * rows)
        p_ref[:, part] = (e_ref[:, part] * c_ref[h : h + 1, :]).astype(BF16)
    term = jnp.dot(p_ref[...], q_ref[...].reshape(heads * rows, -1), preferred_element_type=F32)
    at = 0
    for out in outs:
        n = out.shape[0]
        out[...] = term[at : at + n, :].astype(out.dtype)
        at += n


def first_kernel(part_ref, cross_ref, m_ref, e_ref, q_ref, c_ref, loss_ref, *rest):
    weights(part_ref, cross_ref, m_ref, c_ref, loss_ref)
    products(c_ref, e_ref, q_ref, rest[:-1], rest[-1])


def next_kernel(c_ref, e_ref, q_ref, *rest):
    products(c_ref, e_ref, q_ref, rest[:-1], rest[-1])


def last_kernel(c_ref, in_a_ref, in_b_ref, e_ref, q_ref, out_a_ref, out_b_ref, p_ref):
    products(c_ref, e_ref, q_ref, (out_a_ref, out_b_ref), p_ref)
    out_a_ref[...] += in_a_ref[...].astype(F32)
    out_b_ref[...] += in_b_ref[...].astype(F32)


def grad(small, e, q, size, index, outs):
    heads, rows, width = q.shape
    body = next_kernel if len(small) == 1 else first_kernel if small[-1].dtype == F32 else last_kernel
    made = [(heads, rows), (heads, rows // 2)] if body is first_kernel else []
    shapes = [jax.ShapeDtypeStruct(s, F32) for s in made] + [jax.ShapeDtypeStruct((n, width), d) for n, d in outs]
    return pl.pallas_call(
        body,
        grid=(1,),
        in_specs=[full(*s.shape) for s in small]
        + [pl.BlockSpec((size, heads * rows), lambda _: (index, 0)), full(*q.shape)],
        out_specs=[full(*s.shape) for s in shapes],
        out_shape=shapes,
        scratch_shapes=[pltpu.VMEM((size, heads * rows), BF16)],
        compiler_params=pltpu.CompilerParams(vmem_limit_bytes=(10 + size // 32) * 2**20),
        cost_estimate=pl.CostEstimate(
            flops=2 * size * heads * rows * width,
            bytes_accessed=4 * size * heads * rows + 2 * q.size,
            transcendentals=0,
        ),
    )(*small, e, q)


def shards(nx, nz, user_states, head_gain, item_table, neg_ids, pos_ids, label_mask, seq_len):
    rows, width = user_states.shape
    heads = head_gain.shape[0]
    table_rows = item_table.shape[0]
    neg_dev = neg_ids.shape[0]
    n_dp = nx * nz * lax.axis_size("core")
    factor = neg_dev * n_dp * lax.axis_size("zh") * lax.axis_size("y") / math.sqrt(rows * n_dp)
    x, z = lax.axis_index("x"), lax.axis_index("z")
    offset = (lax.axis_index("zh") * lax.axis_size("y") + lax.axis_index("y")) * table_rows

    def shifted(value, axis, size, by):
        return lax.ppermute(value, axis, [(i, (i + by) % size) for i in range(size)])

    other = shifted(user_states, "core", 2, 1)
    table = shifted(item_table, "core", 2, 1)
    gain = shifted(head_gain, "core", 2, 1)

    slot = lax.broadcasted_iota(jnp.int32, (nx * nz, neg_dev), 0)
    slots = lax.psum(jnp.where(slot == x * nz + z, neg_ids[None], 0), ("x", "z"))

    e, q, m, msg = scores(
        1.0 / math.sqrt(width), nx, nz, x.reshape(1), z.reshape(1), offset.reshape(1), slots, pos_ids,
        gain, user_states, other, table,
    )
    msg = fold(msg, *[lax.ppermute(msg, "y", [(i, i ^ k) for i in range(4)]) for k in (2, 1, 3)])
    part = fold_with_mask(seq_len, label_mask, msg, shifted(msg, "zh", 2, 1))
    cross = shifted(part, "core", 2, 1)

    quarter = nz * neg_dev
    half = quarter // 2
    c, pos_loss, far_a, far_b = grad((part, cross, m), e, q, quarter, 0, [(half, BF16)] * 2)
    far_a, far_b = shifted(far_a, "x", nx, 1), shifted(far_b, "x", nx, -1)
    up_a, up_b, down_a, down_b = grad(
        (c,), e, q, 2 * quarter, 1, [(half, F32), (half, BF16), (half, BF16), (half, F32)]
    )
    up_b, down_a = shifted(up_b, "x", nx, 1), shifted(down_a, "x", nx, -1)
    far_a, far_b = lax.optimization_barrier((far_a, far_b))
    up_a = shifted((up_a + far_a.astype(F32)).astype(BF16), "x", nx, 1)
    down_b = shifted((down_b + far_b.astype(F32)).astype(BF16), "x", nx, -1)
    own_a, own_b = grad((c, down_a, up_b), e, q, quarter, 1, [(half, F32)] * 2)
    total = jnp.concatenate([own_a + up_a.astype(F32), own_b + down_b.astype(F32)], axis=0)

    parts = {k: total[i * neg_dev : (i + 1) * neg_dev] for i, k in enumerate(Z_ORDER)}
    sent = [shifted(parts[k].astype(BF16), "z", nz, k) for k in Z_ORDER if k]
    out = parts[0]
    for piece in sent:
        out = out + piece.astype(F32)
    return pos_loss, out * factor


def solution(mesh):
    nx, nz = 4, 4
    wide = Mesh(mesh.devices.reshape(nx, nz, 2, 2, 4), DP + TOWER)
    placed = (
        P(DP, None),
        P(),
        P(TOWER, None),
        P(DP + TOWER),
        P(DP),
        P(None, DP),
        P(DP),
    )
    return jax.shard_map(
        functools.partial(shards, nx, nz),
        mesh=wide,
        in_specs=placed,
        out_specs=(P(None, DP), P(DP + TOWER, None)),
        check_vma=False,
    )
```

```python
import functools
import math

import jax
import jax.numpy as jnp
from jax import lax
from jax.experimental import pallas as pl
from jax.experimental.pallas import tpu as pltpu
from jax.sharding import Mesh
from jax.sharding import PartitionSpec as P

F32 = jnp.float32
BF16 = jnp.bfloat16
DP = ("x", "z", "core")
TOWER = ("zh", "y")
LOG2E = math.log2(math.e)
NT = (((1,), (1,)), ((), ()))
ORDER = (2, 0, 1, 3)
Z_ORDER = (2, 3, 1, 0)


def full(*shape):
    return pl.BlockSpec(shape, lambda *_: (0,) * len(shape))


def one_hot_rows(ids_row, width):
    column = jnp.broadcast_to(ids_row.astype(F32), (128, 128)).T
    lane = lax.broadcasted_iota(jnp.int32, (128, 128), 1).astype(F32)
    return jnp.concatenate(
        [jnp.where(column == lane + float(v), 1.0, 0.0).astype(BF16) for v in range(0, width, 128)], axis=1
    )


def score_kernel(
    inv, nx, nz, x_ref, z_ref, core_ref, off_ref, ids_ref, pos_ref, pos_other_ref, gain_ref, own_ref, other_ref, table_hbm,
    e_ref, q_ref, m_ref, msg_ref, emb_ref, pos_emb_ref, near_ref, table_ref, sem,
):
    heads = gain_ref.shape[0]
    rows = own_ref.shape[0]
    nd = ids_ref.shape[1]
    width = table_ref.shape[0]
    off = off_ref[0]
    x, z = x_ref[0], z_ref[0]
    copy = pltpu.make_async_copy(table_hbm, table_ref, sem)
    copy.start()
    for head in range(heads):
        gain = gain_ref[head : head + 1, :]
        q_ref[head, :rows, :] = (own_ref[...].astype(F32) * gain).astype(BF16)
        q_ref[head, rows:, :] = (other_ref[...].astype(F32) * gain).astype(BF16)
    copy.wait()
    for b in range(0, nx * nz, 2):
        pair = []
        for i in (b, b + 1):
            rx, rz = ORDER[i // nz], Z_ORDER[i % nz]
            row = lax.rem(x + rx, nx) * nz + lax.rem(z + rz, nz)
            pair.append(ids_ref[pl.ds(row, 1), :] - off)
        hot = one_hot_rows(jnp.concatenate(pair, axis=1), width)
        emb_ref[b * nd : (b + 2) * nd, :] = jnp.dot(hot, table_ref[...], preferred_element_type=F32).astype(BF16)
    one = core_ref[0] == 1
    near_ref[...] = jnp.zeros_like(near_ref)
    pos_ids = [r[a : a + 128].reshape(1, 128) - off for r in (pos_ref, pos_other_ref) for a in range(0, rows, 128)]

    @pl.when(one)
    def _():
        for i, ids in enumerate(pos_ids):
            part = slice(i * 128, i * 128 + 128)
            hot = one_hot_rows(ids, width)
            pos_emb_ref[part, :] = jnp.dot(hot, table_ref[...], preferred_element_type=F32).astype(BF16)
        diag = lax.broadcasted_iota(jnp.int32, (128, 128), 0) == lax.broadcasted_iota(jnp.int32, (128, 128), 1)
        for i in range(len(pos_ids)):
            part = slice(i * 128, i * 128 + 128)
            q = q_ref[:, part, :].reshape(heads * 128, -1)
            d = lax.dot_general(pos_emb_ref[part, :], q, NT, preferred_element_type=F32)
            for head in range(heads):
                mine = jnp.where(diag, d[:, head * 128 : head * 128 + 128], 0.0)
                near_ref[head : head + 1, part] = jnp.sum(mine, axis=0, keepdims=True) * inv

    block = 256
    for head in range(heads):
        for a in range(0, 2 * rows, block):
            s = lax.dot_general(emb_ref[...], q_ref[head, a : a + block, :], NT, preferred_element_type=F32)
            m = jnp.max(s, axis=0, keepdims=True)
            e = jnp.exp2((s - m) * (inv * LOG2E))
            at = head * 2 * rows + a
            e_ref[:, at : at + block] = e
            m_ref[head : head + 1, a : a + block] = m * inv
            msg_ref[head : head + 1, a : a + block] = m * inv + jnp.log(jnp.sum(e, axis=0, keepdims=True))
    for i, ids in enumerate(pos_ids):
        part = slice(i * 128, i * 128 + 128)
        base, pos = msg_ref[:, part], near_ref[:, part]
        owned = (ids >= 0) & (ids < width) & one
        msg_ref[:, part] = jnp.where(owned, pair_sum(base, pos), base)
    msg_ref[:, 2 * rows :] = near_ref[...]


def scores(inv, nx, nz, x, z, core, off, ids, pos, pos_other, gain, own, other, table):
    rows, width = own.shape
    heads = gain.shape[0]
    negs = ids.size
    sm = pl.BlockSpec(memory_space=pltpu.SMEM)
    return pl.pallas_call(
        functools.partial(score_kernel, inv, nx, nz),
        grid=(1,),
        in_specs=[sm, sm, sm, sm, full(*ids.shape), full(*pos.shape), full(*pos.shape), full(*gain.shape),
            full(rows, width), full(rows, width), pl.BlockSpec(memory_space=pl.ANY)],
        out_specs=[
            full(negs, heads * 2 * rows),
            full(heads, 2 * rows, width),
            full(heads, 2 * rows),
            full(heads, 4 * rows),
        ],
        out_shape=[
            jax.ShapeDtypeStruct((negs, heads * 2 * rows), F32),
            jax.ShapeDtypeStruct((heads, 2 * rows, width), BF16),
            jax.ShapeDtypeStruct((heads, 2 * rows), F32),
            jax.ShapeDtypeStruct((heads, 4 * rows), F32),
        ],
        scratch_shapes=[
            pltpu.VMEM((negs, width), BF16),
            pltpu.VMEM((2 * rows, width), BF16),
            pltpu.VMEM((heads, 2 * rows), F32),
            pltpu.VMEM(table.shape, BF16),
            pltpu.SemaphoreType.DMA,
        ],
        compiler_params=pltpu.CompilerParams(vmem_limit_bytes=30 * 2**20),
    )(x, z, core, off, ids, pos, pos_other, gain, own, other, table)


def pair_sum(a, b):
    top = jnp.maximum(a, b)
    return top + jnp.log(jnp.exp(a - top) + jnp.exp(b - top))


def fold_kernel(*refs):
    parts, out_ref = [r[...] for r in refs[:-1]], refs[-1]
    cut = out_ref.shape[1] // 2
    top = functools.reduce(jnp.maximum, [r[:, :cut] for r in parts])
    out_ref[:, :cut] = top + jnp.log(sum(jnp.exp(r[:, :cut] - top) for r in parts))
    out_ref[:, cut:] = sum(r[:, cut:] for r in parts)


def fold(*parts):
    shape = parts[0].shape
    return pl.pallas_call(
        fold_kernel,
        grid=(1,),
        in_specs=[full(*shape)] * len(parts),
        out_specs=full(*shape),
        out_shape=jax.ShapeDtypeStruct(shape, F32),
        compiler_params=pltpu.CompilerParams(vmem_limit_bytes=2**20),
    )(*parts)


def mask_kernel(len_ref, mask_ref, msg_ref, near_ref, out_ref):
    rows = mask_ref.shape[1]
    a, b = msg_ref[...], near_ref[...]
    out_ref[:, : 2 * rows] = pair_sum(a[:, : 2 * rows], b[:, : 2 * rows])
    out_ref[:, 2 * rows : 4 * rows] = a[:, 2 * rows :] + b[:, 2 * rows :]
    valid = lax.broadcasted_iota(jnp.int32, mask_ref.shape, 1) < len_ref[0]
    out_ref[:, 4 * rows :] = jnp.where(valid, mask_ref[...].astype(F32), 0.0)


def fold_with_mask(seq_len, mask, msg, near):
    heads, rows = mask.shape
    return pl.pallas_call(
        mask_kernel,
        grid=(1,),
        in_specs=[pl.BlockSpec(memory_space=pltpu.SMEM), full(*mask.shape), full(*msg.shape), full(*msg.shape)],
        out_specs=full(heads, 5 * rows),
        out_shape=jax.ShapeDtypeStruct((heads, 5 * rows), F32),
        compiler_params=pltpu.CompilerParams(vmem_limit_bytes=2**20),
    )(seq_len, mask, msg, near)


def weights(part_ref, cross_ref, m_ref, c_ref, loss_ref):
    rows = loss_ref.shape[1]
    w = part_ref[:, 4 * rows :]
    lse = pair_sum(part_ref[:, :rows], cross_ref[:, rows : 2 * rows])
    lse_other = pair_sum(part_ref[:, rows : 2 * rows], cross_ref[:, :rows])
    loss_ref[...] = w * (lse - part_ref[:, 2 * rows : 3 * rows] - cross_ref[:, 3 * rows : 4 * rows])
    c_ref[:, :rows] = w * jnp.exp(m_ref[:, :rows] - lse)
    c_ref[:, rows:] = cross_ref[:, 4 * rows :] * jnp.exp(m_ref[:, rows:] - lse_other)


def products(c_ref, e_ref, q_ref, outs, p_ref):
    heads, rows = c_ref.shape
    for h in range(heads):
        part = slice(h * rows, (h + 1) * rows)
        p_ref[:, part] = (e_ref[:, part] * c_ref[h : h + 1, :]).astype(BF16)
    term = jnp.dot(p_ref[...], q_ref[...].reshape(heads * rows, -1), preferred_element_type=F32)
    at = 0
    for out in outs:
        n = out.shape[0]
        out[...] = term[at : at + n, :].astype(out.dtype)
        at += n


def first_kernel(part_ref, cross_ref, m_ref, e_ref, q_ref, c_ref, loss_ref, *rest):
    weights(part_ref, cross_ref, m_ref, c_ref, loss_ref)
    products(c_ref, e_ref, q_ref, rest[:-1], rest[-1])


def next_kernel(c_ref, e_ref, q_ref, *rest):
    products(c_ref, e_ref, q_ref, rest[:-1], rest[-1])


def last_kernel(c_ref, in_a_ref, in_b_ref, e_ref, q_ref, out_a_ref, out_b_ref, p_ref):
    products(c_ref, e_ref, q_ref, (out_a_ref, out_b_ref), p_ref)
    out_a_ref[...] += in_a_ref[...].astype(F32)
    out_b_ref[...] += in_b_ref[...].astype(F32)


def grad(small, e, q, size, index, outs):
    heads, rows, width = q.shape
    body = next_kernel if len(small) == 1 else first_kernel if small[-1].dtype == F32 else last_kernel
    made = [(heads, rows), (heads, rows // 2)] if body is first_kernel else []
    shapes = [jax.ShapeDtypeStruct(s, F32) for s in made] + [jax.ShapeDtypeStruct((n, width), d) for n, d in outs]
    return pl.pallas_call(
        body,
        grid=(1,),
        in_specs=[full(*s.shape) for s in small]
        + [pl.BlockSpec((size, heads * rows), lambda _: (index, 0)), full(*q.shape)],
        out_specs=[full(*s.shape) for s in shapes],
        out_shape=shapes,
        scratch_shapes=[pltpu.VMEM((size, heads * rows), BF16)],
        compiler_params=pltpu.CompilerParams(vmem_limit_bytes=(10 + size // 32) * 2**20),
        cost_estimate=pl.CostEstimate(
            flops=2 * size * heads * rows * width,
            bytes_accessed=4 * size * heads * rows + 2 * q.size,
            transcendentals=0,
        ),
    )(*small, e, q)


def shards(nx, nz, user_states, head_gain, item_table, neg_ids, pos_ids, label_mask, seq_len):
    rows, width = user_states.shape
    heads = head_gain.shape[0]
    table_rows = item_table.shape[0]
    neg_dev = neg_ids.shape[0]
    n_dp = nx * nz * lax.axis_size("core")
    factor = neg_dev * n_dp * lax.axis_size("zh") * lax.axis_size("y") / math.sqrt(rows * n_dp)
    x, z, core = lax.axis_index("x"), lax.axis_index("z"), lax.axis_index("core")
    offset = (lax.axis_index("zh") * lax.axis_size("y") + lax.axis_index("y")) * table_rows

    def shifted(value, axis, size, by):
        return lax.ppermute(value, axis, [(i, (i + by) % size) for i in range(size)])

    other = shifted(user_states, "core", 2, 1)
    table = shifted(item_table, "core", 2, 1)
    gain = shifted(head_gain, "core", 2, 1)
    pos_other = shifted(pos_ids, "core", 2, 1)

    slot = lax.broadcasted_iota(jnp.int32, (nx * nz, neg_dev), 0)
    slots = lax.psum(jnp.where(slot == x * nz + z, neg_ids[None], 0), ("x", "z"))

    e, q, m, msg = scores(
        1.0 / math.sqrt(width), nx, nz, x.reshape(1), z.reshape(1), core.reshape(1), offset.reshape(1), slots, pos_ids, pos_other,
        gain, user_states, other, table,
    )
    msg = fold(msg, *[lax.ppermute(msg, "y", [(i, i ^ k) for i in range(4)]) for k in (2, 1, 3)])
    part = fold_with_mask(seq_len, label_mask, msg, shifted(msg, "zh", 2, 1))
    cross = shifted(part, "core", 2, 1)

    quarter = nz * neg_dev
    half = quarter // 2
    c, pos_loss, far_a, far_b = grad((part, cross, m), e, q, quarter, 0, [(half, BF16)] * 2)
    far_a, far_b = shifted(far_a, "x", nx, 1), shifted(far_b, "x", nx, -1)
    up_a, up_b, down_a, down_b = grad(
        (c,), e, q, 2 * quarter, 1, [(half, F32), (half, BF16), (half, BF16), (half, F32)]
    )
    up_b, down_a = shifted(up_b, "x", nx, 1), shifted(down_a, "x", nx, -1)
    far_a, far_b = lax.optimization_barrier((far_a, far_b))
    up_a = shifted((up_a + far_a.astype(F32)).astype(BF16), "x", nx, 1)
    down_b = shifted((down_b + far_b.astype(F32)).astype(BF16), "x", nx, -1)
    own_a, own_b = grad((c, down_a, up_b), e, q, quarter, 1, [(half, F32)] * 2)
    total = jnp.concatenate([own_a + up_a.astype(F32), own_b + down_b.astype(F32)], axis=0)

    parts = {k: total[i * neg_dev : (i + 1) * neg_dev] for i, k in enumerate(Z_ORDER)}
    sent = [shifted(parts[k].astype(BF16), "z", nz, k) for k in Z_ORDER if k]
    out = parts[0]
    for piece in sent:
        out = out + piece.astype(F32)
    return pos_loss, out * factor


def solution(mesh):
    nx, nz = 4, 4
    wide = Mesh(mesh.devices.reshape(nx, nz, 2, 2, 4), DP + TOWER)
    placed = (
        P(DP, None),
        P(),
        P(TOWER, None),
        P(DP + TOWER),
        P(DP),
        P(None, DP),
        P(DP),
    )
    return jax.shard_map(
        functools.partial(shards, nx, nz),
        mesh=wide,
        in_specs=placed,
        out_specs=(P(None, DP), P(DP + TOWER, None)),
        check_vma=False,
    )
```

```python
import functools
import math

import jax
import jax.numpy as jnp
from jax import lax
from jax.experimental import pallas as pl
from jax.experimental.pallas import tpu as pltpu
from jax.sharding import Mesh
from jax.sharding import PartitionSpec as P

F32 = jnp.float32
BF16 = jnp.bfloat16
DP = ("x", "z", "core")
TOWER = ("zh", "y")
LOG2E = math.log2(math.e)
NT = (((1,), (1,)), ((), ()))
ORDER = (2, 0, 1, 3)
Z_ORDER = (2, 3, 1, 0)


def full(*shape):
    return pl.BlockSpec(shape, lambda *_: (0,) * len(shape))


def one_hot_rows(ids_row, width):
    column = jnp.broadcast_to(ids_row.astype(F32), (128, 128)).T
    lane = lax.broadcasted_iota(jnp.int32, (128, 128), 1).astype(F32)
    return jnp.concatenate(
        [jnp.where(column == lane + float(v), 1.0, 0.0).astype(BF16) for v in range(0, width, 128)], axis=1
    )


def score_kernel(
    inv, nx, nz, x_ref, z_ref, core_ref, off_ref, ids_ref, pos_ref, pos_other_ref, gain_ref, own_ref, other_ref, table_hbm,
    e_ref, q_ref, m_ref, msg_ref, emb_ref, pos_emb_ref, near_ref, table_ref, sem,
):
    heads = gain_ref.shape[0]
    rows = own_ref.shape[0]
    nd = ids_ref.shape[1]
    width = table_ref.shape[0]
    off = off_ref[0]
    x, z = x_ref[0], z_ref[0]
    copy = pltpu.make_async_copy(table_hbm, table_ref, sem)
    copy.start()
    for head in range(heads):
        gain = gain_ref[head : head + 1, :]
        q_ref[head, :rows, :] = (own_ref[...].astype(F32) * gain).astype(BF16)
        q_ref[head, rows:, :] = (other_ref[...].astype(F32) * gain).astype(BF16)
    copy.wait()
    for b in range(0, nx * nz, 2):
        pair = []
        for i in (b, b + 1):
            rx, rz = ORDER[i // nz], Z_ORDER[i % nz]
            row = lax.rem(x + rx, nx) * nz + lax.rem(z + rz, nz)
            pair.append(ids_ref[pl.ds(row, 1), :] - off)
        hot = one_hot_rows(jnp.concatenate(pair, axis=1), width)
        emb_ref[b * nd : (b + 2) * nd, :] = jnp.dot(hot, table_ref[...], preferred_element_type=F32).astype(BF16)
    one = core_ref[0] == 1
    near_ref[...] = jnp.zeros_like(near_ref)
    pos_ids = [r[a : a + 128].reshape(1, 128) - off for r in (pos_ref, pos_other_ref) for a in range(0, rows, 128)]

    @pl.when(one)
    def _():
        for i, ids in enumerate(pos_ids):
            part = slice(i * 128, i * 128 + 128)
            hot = one_hot_rows(ids, width)
            pos_emb_ref[part, :] = jnp.dot(hot, table_ref[...], preferred_element_type=F32).astype(BF16)
        diag = lax.broadcasted_iota(jnp.int32, (128, 128), 0) == lax.broadcasted_iota(jnp.int32, (128, 128), 1)
        for i in range(len(pos_ids)):
            part = slice(i * 128, i * 128 + 128)
            q = q_ref[:, part, :].reshape(heads * 128, -1)
            d = lax.dot_general(pos_emb_ref[part, :], q, NT, preferred_element_type=F32)
            for head in range(heads):
                mine = jnp.where(diag, d[:, head * 128 : head * 128 + 128], 0.0)
                near_ref[head : head + 1, part] = jnp.sum(mine, axis=0, keepdims=True) * inv

    block = 256
    for head in range(heads):
        for a in range(0, 2 * rows, block):
            s = lax.dot_general(emb_ref[...], q_ref[head, a : a + block, :], NT, preferred_element_type=F32)
            m = jnp.max(s, axis=0, keepdims=True)
            e = jnp.exp2((s - m) * (inv * LOG2E))
            at = head * 2 * rows + a
            e_ref[:, at : at + block] = e
            m_ref[head : head + 1, a : a + block] = m * inv
            msg_ref[head : head + 1, a : a + block] = m * inv + jnp.log(jnp.sum(e, axis=0, keepdims=True))
    for i, ids in enumerate(pos_ids):
        part = slice(i * 128, i * 128 + 128)
        base, pos = msg_ref[:, part], near_ref[:, part]
        owned = (ids >= 0) & (ids < width) & one
        msg_ref[:, part] = jnp.where(owned, pair_sum(base, pos), base)
    msg_ref[:, 2 * rows :] = near_ref[...]


def scores(inv, nx, nz, x, z, core, off, ids, pos, pos_other, gain, own, other, table):
    rows, width = own.shape
    heads = gain.shape[0]
    negs = ids.size
    sm = pl.BlockSpec(memory_space=pltpu.SMEM)
    return pl.pallas_call(
        functools.partial(score_kernel, inv, nx, nz),
        grid=(1,),
        in_specs=[sm, sm, sm, sm, full(*ids.shape), full(*pos.shape), full(*pos.shape), full(*gain.shape),
            full(rows, width), full(rows, width), pl.BlockSpec(memory_space=pl.ANY)],
        out_specs=[
            full(negs, heads * 2 * rows),
            full(heads, 2 * rows, width),
            full(heads, 2 * rows),
            full(heads, 4 * rows),
        ],
        out_shape=[
            jax.ShapeDtypeStruct((negs, heads * 2 * rows), F32),
            jax.ShapeDtypeStruct((heads, 2 * rows, width), BF16),
            jax.ShapeDtypeStruct((heads, 2 * rows), F32),
            jax.ShapeDtypeStruct((heads, 4 * rows), F32),
        ],
        scratch_shapes=[
            pltpu.VMEM((negs, width), BF16),
            pltpu.VMEM((2 * rows, width), BF16),
            pltpu.VMEM((heads, 2 * rows), F32),
            pltpu.VMEM(table.shape, BF16),
            pltpu.SemaphoreType.DMA,
        ],
        compiler_params=pltpu.CompilerParams(vmem_limit_bytes=30 * 2**20),
    )(x, z, core, off, ids, pos, pos_other, gain, own, other, table)


def pair_sum(a, b):
    top = jnp.maximum(a, b)
    return top + jnp.log(jnp.exp(a - top) + jnp.exp(b - top))


def fold_kernel(*refs):
    parts, out_ref = [r[...] for r in refs[:-1]], refs[-1]
    cut = out_ref.shape[1] // 2
    top = functools.reduce(jnp.maximum, [r[:, :cut] for r in parts])
    out_ref[:, :cut] = top + jnp.log(sum(jnp.exp(r[:, :cut] - top) for r in parts))
    out_ref[:, cut:] = sum(r[:, cut:] for r in parts)


def fold(*parts):
    shape = parts[0].shape
    return pl.pallas_call(
        fold_kernel,
        grid=(1,),
        in_specs=[full(*shape)] * len(parts),
        out_specs=full(*shape),
        out_shape=jax.ShapeDtypeStruct(shape, F32),
        compiler_params=pltpu.CompilerParams(vmem_limit_bytes=2**20),
    )(*parts)


def mask_kernel(len_ref, mask_ref, msg_ref, near_ref, out_ref):
    rows = mask_ref.shape[1]
    a, b = msg_ref[...], near_ref[...]
    out_ref[:, : 2 * rows] = pair_sum(a[:, : 2 * rows], b[:, : 2 * rows])
    out_ref[:, 2 * rows : 4 * rows] = a[:, 2 * rows :] + b[:, 2 * rows :]
    valid = lax.broadcasted_iota(jnp.int32, mask_ref.shape, 1) < len_ref[0]
    out_ref[:, 4 * rows :] = jnp.where(valid, mask_ref[...].astype(F32), 0.0)


def fold_with_mask(seq_len, mask, msg, near):
    heads, rows = mask.shape
    return pl.pallas_call(
        mask_kernel,
        grid=(1,),
        in_specs=[pl.BlockSpec(memory_space=pltpu.SMEM), full(*mask.shape), full(*msg.shape), full(*msg.shape)],
        out_specs=full(heads, 5 * rows),
        out_shape=jax.ShapeDtypeStruct((heads, 5 * rows), F32),
        compiler_params=pltpu.CompilerParams(vmem_limit_bytes=2**20),
    )(seq_len, mask, msg, near)


def weights(part_ref, cross_ref, m_ref, c_ref, loss_ref):
    rows = loss_ref.shape[1]
    w = part_ref[:, 4 * rows :]
    lse = pair_sum(part_ref[:, :rows], cross_ref[:, rows : 2 * rows])
    lse_other = pair_sum(part_ref[:, rows : 2 * rows], cross_ref[:, :rows])
    loss_ref[...] = w * (lse - part_ref[:, 2 * rows : 3 * rows] - cross_ref[:, 3 * rows : 4 * rows])
    c_ref[:, :rows] = w * jnp.exp(m_ref[:, :rows] - lse)
    c_ref[:, rows:] = cross_ref[:, 4 * rows :] * jnp.exp(m_ref[:, rows:] - lse_other)


def products(c_ref, e_ref, q_ref, outs, p_ref):
    heads, rows = c_ref.shape
    for h in range(heads):
        part = slice(h * rows, (h + 1) * rows)
        p_ref[:, part] = (e_ref[:, part] * c_ref[h : h + 1, :]).astype(BF16)
    term = jnp.dot(p_ref[...], q_ref[...].reshape(heads * rows, -1), preferred_element_type=F32)
    at = 0
    for out in outs:
        n = out.shape[0]
        out[...] = term[at : at + n, :].astype(out.dtype)
        at += n


def first_kernel(part_ref, cross_ref, m_ref, e_ref, q_ref, c_ref, loss_ref, *rest):
    weights(part_ref, cross_ref, m_ref, c_ref, loss_ref)
    products(c_ref, e_ref, q_ref, rest[:-1], rest[-1])


def next_kernel(c_ref, e_ref, q_ref, *rest):
    products(c_ref, e_ref, q_ref, rest[:-1], rest[-1])


def last_kernel(c_ref, in_a_ref, in_b_ref, e_ref, q_ref, out_a_ref, out_b_ref, p_ref):
    products(c_ref, e_ref, q_ref, (out_a_ref, out_b_ref), p_ref)
    out_a_ref[...] += in_a_ref[...].astype(F32)
    out_b_ref[...] += in_b_ref[...].astype(F32)


def grad(small, e, q, size, index, outs):
    heads, rows, width = q.shape
    body = next_kernel if len(small) == 1 else first_kernel if small[-1].dtype == F32 else last_kernel
    made = [(heads, rows), (heads, rows // 2)] if body is first_kernel else []
    shapes = [jax.ShapeDtypeStruct(s, F32) for s in made] + [jax.ShapeDtypeStruct((n, width), d) for n, d in outs]
    return pl.pallas_call(
        body,
        grid=(1,),
        in_specs=[full(*s.shape) for s in small]
        + [pl.BlockSpec((size, heads * rows), lambda _: (index, 0)), full(*q.shape)],
        out_specs=[full(*s.shape) for s in shapes],
        out_shape=shapes,
        scratch_shapes=[pltpu.VMEM((size, heads * rows), BF16)],
        compiler_params=pltpu.CompilerParams(vmem_limit_bytes=(10 + size // 32) * 2**20),
        cost_estimate=pl.CostEstimate(
            flops=2 * size * heads * rows * width,
            bytes_accessed=4 * size * heads * rows + 2 * q.size,
            transcendentals=0,
        ),
    )(*small, e, q)


def shards(nx, nz, user_states, head_gain, item_table, neg_ids, pos_ids, label_mask, seq_len):
    rows, width = user_states.shape
    heads = head_gain.shape[0]
    table_rows = item_table.shape[0]
    neg_dev = neg_ids.shape[0]
    n_dp = nx * nz * lax.axis_size("core")
    factor = neg_dev * n_dp * lax.axis_size("zh") * lax.axis_size("y") / math.sqrt(rows * n_dp)
    x, z, core = lax.axis_index("x"), lax.axis_index("z"), lax.axis_index("core")
    offset = (lax.axis_index("zh") * lax.axis_size("y") + lax.axis_index("y")) * table_rows

    def shifted(value, axis, size, by):
        return lax.ppermute(value, axis, [(i, (i + by) % size) for i in range(size)])

    other = shifted(user_states, "core", 2, 1)
    own, table, gain = (shifted(v, "core", 2, 0) for v in (user_states, item_table, head_gain))
    pos_other = shifted(pos_ids, "core", 2, 1)

    slot = lax.broadcasted_iota(jnp.int32, (nx * nz, neg_dev), 0)
    slots = lax.psum(jnp.where(slot == x * nz + z, neg_ids[None], 0), ("x", "z"))

    e, q, m, msg = scores(
        1.0 / math.sqrt(width), nx, nz, x.reshape(1), z.reshape(1), core.reshape(1), offset.reshape(1), slots, pos_ids, pos_other,
        gain, own, other, table,
    )
    msg = fold(msg, *[lax.ppermute(msg, "y", [(i, i ^ k) for i in range(4)]) for k in (2, 1, 3)])
    part = fold_with_mask(seq_len, label_mask, msg, shifted(msg, "zh", 2, 1))
    cross = shifted(part, "core", 2, 1)

    quarter = nz * neg_dev
    half = quarter // 2
    c, pos_loss, far_a, far_b = grad((part, cross, m), e, q, quarter, 0, [(half, BF16)] * 2)
    far_a, far_b = shifted(far_a, "x", nx, 1), shifted(far_b, "x", nx, -1)
    up_a, up_b, down_a, down_b = grad(
        (c,), e, q, 2 * quarter, 1, [(half, F32), (half, BF16), (half, BF16), (half, F32)]
    )
    up_b, down_a = shifted(up_b, "x", nx, 1), shifted(down_a, "x", nx, -1)
    far_a, far_b = lax.optimization_barrier((far_a, far_b))
    up_a = shifted((up_a + far_a.astype(F32)).astype(BF16), "x", nx, 1)
    down_b = shifted((down_b + far_b.astype(F32)).astype(BF16), "x", nx, -1)
    own_a, own_b = grad((c, down_a, up_b), e, q, quarter, 1, [(half, F32)] * 2)
    total = jnp.concatenate([own_a + up_a.astype(F32), own_b + down_b.astype(F32)], axis=0)

    parts = {k: total[i * neg_dev : (i + 1) * neg_dev] for i, k in enumerate(Z_ORDER)}
    sent = [shifted(parts[k].astype(BF16), "z", nz, k) for k in Z_ORDER if k]
    out = parts[0]
    for piece in sent:
        out = out + piece.astype(F32)
    return pos_loss, out * factor


def solution(mesh):
    nx, nz = 4, 4
    wide = Mesh(mesh.devices.reshape(nx, nz, 2, 2, 4), DP + TOWER)
    placed = (
        P(DP, None),
        P(),
        P(TOWER, None),
        P(DP + TOWER),
        P(DP),
        P(None, DP),
        P(DP),
    )
    return jax.shard_map(
        functools.partial(shards, nx, nz),
        mesh=wide,
        in_specs=placed,
        out_specs=(P(None, DP), P(DP + TOWER, None)),
        check_vma=False,
    )
```

```python
import functools
import math

import jax
import jax.numpy as jnp
from jax import lax
from jax.experimental import pallas as pl
from jax.experimental.pallas import tpu as pltpu
from jax.sharding import Mesh
from jax.sharding import PartitionSpec as P

F32 = jnp.float32
BF16 = jnp.bfloat16
DP = ("x", "z", "core")
TOWER = ("zh", "y")
LOG2E = math.log2(math.e)
NT = (((1,), (1,)), ((), ()))
ORDER = (2, 0, 1, 3)
Z_ORDER = (2, 3, 1, 0)


def full(*shape):
    return pl.BlockSpec(shape, lambda *_: (0,) * len(shape))


def one_hot_rows(ids_row, width):
    column = jnp.broadcast_to(ids_row.astype(F32), (128, 128)).T
    lane = lax.broadcasted_iota(jnp.int32, (128, 128), 1).astype(F32)
    return jnp.concatenate(
        [jnp.where(column == lane + float(v), 1.0, 0.0).astype(BF16) for v in range(0, width, 128)], axis=1
    )


def score_kernel(
    inv, nx, nz, x_ref, z_ref, core_ref, off_ref, ids_ref, pos_ref, pos_other_ref, gain_ref, own_ref, other_ref, table_hbm,
    e_ref, q_ref, m_ref, msg_ref, emb_ref, pos_emb_ref, near_ref, table_ref, sem,
):
    heads = gain_ref.shape[0]
    rows = own_ref.shape[0]
    nd = ids_ref.shape[1]
    width = table_ref.shape[0]
    off = off_ref[0]
    x, z = x_ref[0], z_ref[0]
    copy = pltpu.make_async_copy(table_hbm, table_ref, sem)
    copy.start()
    for head in range(heads):
        gain = gain_ref[head : head + 1, :]
        q_ref[head, :rows, :] = (own_ref[...].astype(F32) * gain).astype(BF16)
        q_ref[head, rows:, :] = (other_ref[...].astype(F32) * gain).astype(BF16)
    copy.wait()
    for b in range(0, nx * nz, 2):
        pair = []
        for i in (b, b + 1):
            rx, rz = ORDER[i // nz], Z_ORDER[i % nz]
            row = lax.rem(x + rx, nx) * nz + lax.rem(z + rz, nz)
            pair.append(ids_ref[pl.ds(row, 1), :] - off)
        hot = one_hot_rows(jnp.concatenate(pair, axis=1), width)
        emb_ref[b * nd : (b + 2) * nd, :] = jnp.dot(hot, table_ref[...], preferred_element_type=F32).astype(BF16)
    one = core_ref[0] == 1
    near_ref[...] = jnp.zeros_like(near_ref)
    pos_ids = [r[a : a + 128].reshape(1, 128) - off for r in (pos_ref, pos_other_ref) for a in range(0, rows, 128)]

    @pl.when(one)
    def _():
        for i, ids in enumerate(pos_ids):
            part = slice(i * 128, i * 128 + 128)
            hot = one_hot_rows(ids, width)
            pos_emb_ref[part, :] = jnp.dot(hot, table_ref[...], preferred_element_type=F32).astype(BF16)
        diag = lax.broadcasted_iota(jnp.int32, (128, 128), 0) == lax.broadcasted_iota(jnp.int32, (128, 128), 1)
        for i in range(len(pos_ids)):
            part = slice(i * 128, i * 128 + 128)
            q = q_ref[:, part, :].reshape(heads * 128, -1)
            d = lax.dot_general(pos_emb_ref[part, :], q, NT, preferred_element_type=F32)
            for head in range(heads):
                mine = jnp.where(diag, d[:, head * 128 : head * 128 + 128], 0.0)
                near_ref[head : head + 1, part] = jnp.sum(mine, axis=0, keepdims=True) * inv

    block = 256
    for head in range(heads):
        for a in range(0, 2 * rows, block):
            s = lax.dot_general(emb_ref[...], q_ref[head, a : a + block, :], NT, preferred_element_type=F32)
            m = jnp.max(s, axis=0, keepdims=True)
            e = jnp.exp2((s - m) * (inv * LOG2E))
            at = head * 2 * rows + a
            e_ref[:, at : at + block] = e
            m_ref[head : head + 1, a : a + block] = m * inv
            msg_ref[head : head + 1, a : a + block] = m * inv + jnp.log(jnp.sum(e, axis=0, keepdims=True))
    for i, ids in enumerate(pos_ids):
        part = slice(i * 128, i * 128 + 128)
        base, pos = msg_ref[:, part], near_ref[:, part]
        owned = (ids >= 0) & (ids < width) & one
        msg_ref[:, part] = jnp.where(owned, pair_sum(base, pos), base)
    msg_ref[:, 2 * rows :] = near_ref[...]


def scores(inv, nx, nz, x, z, core, off, ids, pos, pos_other, gain, own, other, table):
    rows, width = own.shape
    heads = gain.shape[0]
    negs = ids.size
    sm = pl.BlockSpec(memory_space=pltpu.SMEM)
    return pl.pallas_call(
        functools.partial(score_kernel, inv, nx, nz),
        grid=(1,),
        in_specs=[sm, sm, sm, sm, full(*ids.shape), full(*pos.shape), full(*pos.shape), full(*gain.shape),
            full(rows, width), full(rows, width), pl.BlockSpec(memory_space=pl.ANY)],
        out_specs=[
            full(negs, heads * 2 * rows),
            full(heads, 2 * rows, width),
            full(heads, 2 * rows),
            full(heads, 4 * rows),
        ],
        out_shape=[
            jax.ShapeDtypeStruct((negs, heads * 2 * rows), F32),
            jax.ShapeDtypeStruct((heads, 2 * rows, width), BF16),
            jax.ShapeDtypeStruct((heads, 2 * rows), F32),
            jax.ShapeDtypeStruct((heads, 4 * rows), F32),
        ],
        scratch_shapes=[
            pltpu.VMEM((negs, width), BF16),
            pltpu.VMEM((2 * rows, width), BF16),
            pltpu.VMEM((heads, 2 * rows), F32),
            pltpu.VMEM(table.shape, BF16),
            pltpu.SemaphoreType.DMA,
        ],
        compiler_params=pltpu.CompilerParams(vmem_limit_bytes=30 * 2**20),
    )(x, z, core, off, ids, pos, pos_other, gain, own, other, table)


def pair_sum(a, b):
    top = jnp.maximum(a, b)
    return top + jnp.log(jnp.exp(a - top) + jnp.exp(b - top))


def fold_kernel(*refs):
    parts, out_ref = [r[...] for r in refs[:-1]], refs[-1]
    cut = out_ref.shape[1] // 2
    top = functools.reduce(jnp.maximum, [r[:, :cut] for r in parts])
    out_ref[:, :cut] = top + jnp.log(sum(jnp.exp(r[:, :cut] - top) for r in parts))
    out_ref[:, cut:] = sum(r[:, cut:] for r in parts)


def fold(*parts):
    shape = parts[0].shape
    return pl.pallas_call(
        fold_kernel,
        grid=(1,),
        in_specs=[full(*shape)] * len(parts),
        out_specs=full(*shape),
        out_shape=jax.ShapeDtypeStruct(shape, F32),
        compiler_params=pltpu.CompilerParams(vmem_limit_bytes=2**20),
    )(*parts)


def mask_kernel(len_ref, mask_ref, msg_ref, near_ref, out_ref):
    rows = mask_ref.shape[1]
    a, b = msg_ref[...], near_ref[...]
    out_ref[:, : 2 * rows] = pair_sum(a[:, : 2 * rows], b[:, : 2 * rows])
    out_ref[:, 2 * rows : 4 * rows] = a[:, 2 * rows :] + b[:, 2 * rows :]
    valid = lax.broadcasted_iota(jnp.int32, mask_ref.shape, 1) < len_ref[0]
    out_ref[:, 4 * rows :] = jnp.where(valid, mask_ref[...].astype(F32), 0.0)


def fold_with_mask(seq_len, mask, msg, near):
    heads, rows = mask.shape
    return pl.pallas_call(
        mask_kernel,
        grid=(1,),
        in_specs=[pl.BlockSpec(memory_space=pltpu.SMEM), full(*mask.shape), full(*msg.shape), full(*msg.shape)],
        out_specs=full(heads, 5 * rows),
        out_shape=jax.ShapeDtypeStruct((heads, 5 * rows), F32),
        compiler_params=pltpu.CompilerParams(vmem_limit_bytes=2**20),
    )(seq_len, mask, msg, near)


def weights(part_ref, cross_ref, m_ref, c_ref, loss_ref):
    rows = loss_ref.shape[1]
    w = part_ref[:, 4 * rows :]
    lse = pair_sum(part_ref[:, :rows], cross_ref[:, rows : 2 * rows])
    lse_other = pair_sum(part_ref[:, rows : 2 * rows], cross_ref[:, :rows])
    loss_ref[...] = w * (lse - part_ref[:, 2 * rows : 3 * rows] - cross_ref[:, 3 * rows : 4 * rows])
    c_ref[:, :rows] = w * jnp.exp(m_ref[:, :rows] - lse)
    c_ref[:, rows:] = cross_ref[:, 4 * rows :] * jnp.exp(m_ref[:, rows:] - lse_other)


def products(c_ref, e_ref, q_ref, outs, p_ref):
    heads, rows = c_ref.shape
    for h in range(heads):
        part = slice(h * rows, (h + 1) * rows)
        p_ref[:, part] = (e_ref[:, part] * c_ref[h : h + 1, :]).astype(BF16)
    term = jnp.dot(p_ref[...], q_ref[...].reshape(heads * rows, -1), preferred_element_type=F32)
    at = 0
    for out in outs:
        n = out.shape[0]
        out[...] = term[at : at + n, :].astype(out.dtype)
        at += n


def first_kernel(part_ref, cross_ref, m_ref, e_ref, q_ref, c_ref, loss_ref, *rest):
    weights(part_ref, cross_ref, m_ref, c_ref, loss_ref)
    products(c_ref, e_ref, q_ref, rest[:-1], rest[-1])


def next_kernel(c_ref, e_ref, q_ref, *rest):
    products(c_ref, e_ref, q_ref, rest[:-1], rest[-1])


def last_kernel(c_ref, in_a_ref, in_b_ref, e_ref, q_ref, out_a_ref, out_b_ref, p_ref):
    products(c_ref, e_ref, q_ref, (out_a_ref, out_b_ref), p_ref)
    out_a_ref[...] += in_a_ref[...].astype(F32)
    out_b_ref[...] += in_b_ref[...].astype(F32)


def grad(small, e, q, size, index, outs):
    heads, rows, width = q.shape
    body = next_kernel if len(small) == 1 else first_kernel if small[-1].dtype == F32 else last_kernel
    made = [(heads, rows), (heads, rows // 2)] if body is first_kernel else []
    shapes = [jax.ShapeDtypeStruct(s, F32) for s in made] + [jax.ShapeDtypeStruct((n, width), d) for n, d in outs]
    return pl.pallas_call(
        body,
        grid=(1,),
        in_specs=[full(*s.shape) for s in small]
        + [pl.BlockSpec((size, heads * rows), lambda _: (index, 0)), full(*q.shape)],
        out_specs=[full(*s.shape) for s in shapes],
        out_shape=shapes,
        scratch_shapes=[pltpu.VMEM((size, heads * rows), BF16)],
        compiler_params=pltpu.CompilerParams(vmem_limit_bytes=(10 + size // 32) * 2**20),
        cost_estimate=pl.CostEstimate(
            flops=2 * size * heads * rows * width,
            bytes_accessed=4 * size * heads * rows + 2 * q.size,
            transcendentals=0,
        ),
    )(*small, e, q)


def shards(nx, nz, user_states, head_gain, item_table, neg_ids, pos_ids, label_mask, seq_len):
    rows, width = user_states.shape
    heads = head_gain.shape[0]
    table_rows = item_table.shape[0]
    neg_dev = neg_ids.shape[0]
    n_dp = nx * nz * lax.axis_size("core")
    factor = neg_dev * n_dp * lax.axis_size("zh") * lax.axis_size("y") / math.sqrt(rows * n_dp)
    x, z, core = lax.axis_index("x"), lax.axis_index("z"), lax.axis_index("core")
    offset = (lax.axis_index("zh") * lax.axis_size("y") + lax.axis_index("y")) * table_rows

    def shifted(value, axis, size, by):
        return lax.ppermute(value, axis, [(i, (i + by) % size) for i in range(size)])

    other = shifted(user_states, "core", 2, 1)
    table = shifted(item_table, "core", 2, 1)
    gain = shifted(head_gain, "core", 2, 1)
    pos_other = shifted(pos_ids, "core", 2, 1)
    pos_near = shifted(pos_ids, "y", 4, 1)

    slot = lax.broadcasted_iota(jnp.int32, (nx * nz, neg_dev), 0)
    slots = lax.psum(jnp.where(slot == x * nz + z, neg_ids[None], 0), ("x", "z"))

    e, q, m, msg = scores(
        1.0 / math.sqrt(width), nx, nz, x.reshape(1), z.reshape(1), core.reshape(1), offset.reshape(1), slots, pos_near, pos_other,
        gain, user_states, other, table,
    )
    msg = fold(msg, *[lax.ppermute(msg, "y", [(i, i ^ k) for i in range(4)]) for k in (2, 1, 3)])
    part = fold_with_mask(seq_len, label_mask, msg, shifted(msg, "zh", 2, 1))
    cross = shifted(part, "core", 2, 1)

    quarter = nz * neg_dev
    half = quarter // 2
    c, pos_loss, far_a, far_b = grad((part, cross, m), e, q, quarter, 0, [(half, BF16)] * 2)
    far_a, far_b = shifted(far_a, "x", nx, 1), shifted(far_b, "x", nx, -1)
    up_a, up_b, down_a, down_b = grad(
        (c,), e, q, 2 * quarter, 1, [(half, F32), (half, BF16), (half, BF16), (half, F32)]
    )
    up_b, down_a = shifted(up_b, "x", nx, 1), shifted(down_a, "x", nx, -1)
    far_a, far_b = lax.optimization_barrier((far_a, far_b))
    up_a = shifted((up_a + far_a.astype(F32)).astype(BF16), "x", nx, 1)
    down_b = shifted((down_b + far_b.astype(F32)).astype(BF16), "x", nx, -1)
    own_a, own_b = grad((c, down_a, up_b), e, q, quarter, 1, [(half, F32)] * 2)
    total = jnp.concatenate([own_a + up_a.astype(F32), own_b + down_b.astype(F32)], axis=0)

    parts = {k: total[i * neg_dev : (i + 1) * neg_dev] for i, k in enumerate(Z_ORDER)}
    sent = [shifted(parts[k].astype(BF16), "z", nz, k) for k in Z_ORDER if k]
    out = parts[0]
    for piece in sent:
        out = out + piece.astype(F32)
    return pos_loss, out * factor


def solution(mesh):
    nx, nz = 4, 4
    wide = Mesh(mesh.devices.reshape(nx, nz, 2, 2, 4), DP + TOWER)
    placed = (
        P(DP, None),
        P(),
        P(TOWER, None),
        P(DP + TOWER),
        P(DP),
        P(None, DP),
        P(DP),
    )
    return jax.shard_map(
        functools.partial(shards, nx, nz),
        mesh=wide,
        in_specs=placed,
        out_specs=(P(None, DP), P(DP + TOWER, None)),
        check_vma=False,
    )
```

```python
import functools
import math

import jax
import jax.numpy as jnp
from jax import lax
from jax.experimental import pallas as pl
from jax.experimental.pallas import tpu as pltpu
from jax.sharding import Mesh
from jax.sharding import PartitionSpec as P

F32 = jnp.float32
BF16 = jnp.bfloat16
DP = ("x", "z", "core")
TOWER = ("zh", "y")
LOG2E = math.log2(math.e)
NT = (((1,), (1,)), ((), ()))
ORDER = (2, 0, 1, 3)
Z_ORDER = (2, 3, 1, 0)


def full(*shape):
    return pl.BlockSpec(shape, lambda *_: (0,) * len(shape))


def one_hot_rows(ids_row, width):
    column = jnp.broadcast_to(ids_row.astype(F32), (128, 128)).T
    lane = lax.broadcasted_iota(jnp.int32, (128, 128), 1).astype(F32)
    return jnp.concatenate(
        [jnp.where(column == lane + float(v), 1.0, 0.0).astype(BF16) for v in range(0, width, 128)], axis=1
    )


def score_kernel(
    inv, nx, nz, x_ref, z_ref, core_ref, off_ref, ids_ref, pos_ref, pos_other_ref, gain_ref, own_ref, other_ref, table_hbm,
    e_ref, q_ref, m_ref, msg_ref, emb_ref, pos_emb_ref, near_ref, table_ref, sem,
):
    heads = gain_ref.shape[0]
    rows = own_ref.shape[0]
    nd = ids_ref.shape[1]
    width = table_ref.shape[0]
    off = off_ref[0]
    x, z = x_ref[0], z_ref[0]
    copy = pltpu.make_async_copy(table_hbm, table_ref, sem)
    copy.start()
    for head in range(heads):
        gain = gain_ref[head : head + 1, :]
        q_ref[head, :rows, :] = (own_ref[...].astype(F32) * gain).astype(BF16)
        q_ref[head, rows:, :] = (other_ref[...].astype(F32) * gain).astype(BF16)
    copy.wait()
    for b in range(0, nx * nz, 2):
        pair = []
        for i in (b, b + 1):
            rx, rz = ORDER[i // nz], Z_ORDER[i % nz]
            row = lax.rem(x + rx, nx) * nz + lax.rem(z + rz, nz)
            pair.append(ids_ref[pl.ds(row, 1), :] - off)
        hot = one_hot_rows(jnp.concatenate(pair, axis=1), width)
        emb_ref[b * nd : (b + 2) * nd, :] = jnp.dot(hot, table_ref[...], preferred_element_type=F32).astype(BF16)
    one = core_ref[0] == 1
    near_ref[...] = jnp.zeros_like(near_ref)
    pos_ids = [r[a : a + 128].reshape(1, 128) - off for r in (pos_ref, pos_other_ref) for a in range(0, rows, 128)]

    @pl.when(one)
    def _():
        for i, ids in enumerate(pos_ids):
            part = slice(i * 128, i * 128 + 128)
            hot = one_hot_rows(ids, width)
            pos_emb_ref[part, :] = jnp.dot(hot, table_ref[...], preferred_element_type=F32).astype(BF16)
        diag = lax.broadcasted_iota(jnp.int32, (128, 128), 0) == lax.broadcasted_iota(jnp.int32, (128, 128), 1)
        for i in range(len(pos_ids)):
            part = slice(i * 128, i * 128 + 128)
            q = q_ref[:, part, :].reshape(heads * 128, -1)
            d = lax.dot_general(pos_emb_ref[part, :], q, NT, preferred_element_type=F32)
            for head in range(heads):
                mine = jnp.where(diag, d[:, head * 128 : head * 128 + 128], 0.0)
                near_ref[head : head + 1, part] = jnp.sum(mine, axis=0, keepdims=True) * inv

    block = 256
    for head in range(heads):
        for a in range(0, 2 * rows, block):
            s = lax.dot_general(emb_ref[...], q_ref[head, a : a + block, :], NT, preferred_element_type=F32)
            m = jnp.max(s, axis=0, keepdims=True)
            e = jnp.exp2((s - m) * (inv * LOG2E))
            at = head * 2 * rows + a
            e_ref[:, at : at + block] = e
            m_ref[head : head + 1, a : a + block] = m * inv
            msg_ref[head : head + 1, a : a + block] = m * inv + jnp.log(jnp.sum(e, axis=0, keepdims=True))
    for i, ids in enumerate(pos_ids):
        part = slice(i * 128, i * 128 + 128)
        base, pos = msg_ref[:, part], near_ref[:, part]
        owned = (ids >= 0) & (ids < width) & one
        msg_ref[:, part] = jnp.where(owned, pair_sum(base, pos), base)
    msg_ref[:, 2 * rows :] = near_ref[...]


def scores(inv, nx, nz, x, z, core, off, ids, pos, pos_other, gain, own, other, table):
    rows, width = own.shape
    heads = gain.shape[0]
    negs = ids.size
    sm = pl.BlockSpec(memory_space=pltpu.SMEM)
    return pl.pallas_call(
        functools.partial(score_kernel, inv, nx, nz),
        grid=(1,),
        in_specs=[sm, sm, sm, sm, full(*ids.shape), full(*pos.shape), full(*pos.shape), full(*gain.shape),
            full(rows, width), full(rows, width), pl.BlockSpec(memory_space=pl.ANY)],
        out_specs=[
            full(negs, heads * 2 * rows),
            full(heads, 2 * rows, width),
            full(heads, 2 * rows),
            full(heads, 4 * rows),
        ],
        out_shape=[
            jax.ShapeDtypeStruct((negs, heads * 2 * rows), F32),
            jax.ShapeDtypeStruct((heads, 2 * rows, width), BF16),
            jax.ShapeDtypeStruct((heads, 2 * rows), F32),
            jax.ShapeDtypeStruct((heads, 4 * rows), F32),
        ],
        scratch_shapes=[
            pltpu.VMEM((negs, width), BF16),
            pltpu.VMEM((2 * rows, width), BF16),
            pltpu.VMEM((heads, 2 * rows), F32),
            pltpu.VMEM(table.shape, BF16),
            pltpu.SemaphoreType.DMA,
        ],
        compiler_params=pltpu.CompilerParams(vmem_limit_bytes=30 * 2**20),
    )(x, z, core, off, ids, pos, pos_other, gain, own, other, table)


def pair_sum(a, b):
    top = jnp.maximum(a, b)
    return top + jnp.log(jnp.exp(a - top) + jnp.exp(b - top))


def fold_kernel(*refs):
    parts, out_ref = [r[...] for r in refs[:-1]], refs[-1]
    cut = out_ref.shape[1] // 2
    top = functools.reduce(jnp.maximum, [r[:, :cut] for r in parts])
    out_ref[:, :cut] = top + jnp.log(sum(jnp.exp(r[:, :cut] - top) for r in parts))
    out_ref[:, cut:] = sum(r[:, cut:] for r in parts)


def fold(*parts):
    shape = parts[0].shape
    return pl.pallas_call(
        fold_kernel,
        grid=(1,),
        in_specs=[full(*shape)] * len(parts),
        out_specs=full(*shape),
        out_shape=jax.ShapeDtypeStruct(shape, F32),
        compiler_params=pltpu.CompilerParams(vmem_limit_bytes=2**20),
    )(*parts)


def mask_kernel(len_ref, mask_ref, msg_ref, near_ref, out_ref):
    rows = mask_ref.shape[1]
    a, b = msg_ref[...], near_ref[...]
    out_ref[:, : 2 * rows] = pair_sum(a[:, : 2 * rows], b[:, : 2 * rows])
    out_ref[:, 2 * rows : 4 * rows] = a[:, 2 * rows :] + b[:, 2 * rows :]
    valid = lax.broadcasted_iota(jnp.int32, mask_ref.shape, 1) < len_ref[0]
    out_ref[:, 4 * rows :] = jnp.where(valid, mask_ref[...].astype(F32), 0.0)


def fold_with_mask(seq_len, mask, msg, near):
    heads, rows = mask.shape
    return pl.pallas_call(
        mask_kernel,
        grid=(1,),
        in_specs=[pl.BlockSpec(memory_space=pltpu.SMEM), full(*mask.shape), full(*msg.shape), full(*msg.shape)],
        out_specs=full(heads, 5 * rows),
        out_shape=jax.ShapeDtypeStruct((heads, 5 * rows), F32),
        compiler_params=pltpu.CompilerParams(vmem_limit_bytes=2**20),
    )(seq_len, mask, msg, near)


def weights(part_ref, cross_ref, m_ref, c_ref, loss_ref):
    rows = loss_ref.shape[1]
    w = part_ref[:, 4 * rows :]
    lse = pair_sum(part_ref[:, :rows], cross_ref[:, rows : 2 * rows])
    lse_other = pair_sum(part_ref[:, rows : 2 * rows], cross_ref[:, :rows])
    loss_ref[...] = w * (lse - part_ref[:, 2 * rows : 3 * rows] - cross_ref[:, 3 * rows : 4 * rows])
    c_ref[:, :rows] = w * jnp.exp(m_ref[:, :rows] - lse)
    c_ref[:, rows:] = cross_ref[:, 4 * rows :] * jnp.exp(m_ref[:, rows:] - lse_other)


def products(c_ref, e_ref, q_ref, outs, p_ref):
    heads, rows = c_ref.shape
    for h in range(heads):
        part = slice(h * rows, (h + 1) * rows)
        p_ref[:, part] = (e_ref[:, part] * c_ref[h : h + 1, :]).astype(BF16)
    term = jnp.dot(p_ref[...], q_ref[...].reshape(heads * rows, -1), preferred_element_type=F32)
    at = 0
    for out in outs:
        n = out.shape[0]
        out[...] = term[at : at + n, :].astype(out.dtype)
        at += n


def first_kernel(part_ref, cross_ref, m_ref, e_ref, q_ref, c_ref, loss_ref, *rest):
    weights(part_ref, cross_ref, m_ref, c_ref, loss_ref)
    products(c_ref, e_ref, q_ref, rest[:-1], rest[-1])


def next_kernel(c_ref, e_ref, q_ref, *rest):
    products(c_ref, e_ref, q_ref, rest[:-1], rest[-1])


def last_kernel(c_ref, in_a_ref, in_b_ref, e_ref, q_ref, out_a_ref, out_b_ref, p_ref):
    products(c_ref, e_ref, q_ref, (out_a_ref, out_b_ref), p_ref)
    out_a_ref[...] += in_a_ref[...].astype(F32)
    out_b_ref[...] += in_b_ref[...].astype(F32)


def grad(small, e, q, size, index, outs):
    heads, rows, width = q.shape
    body = next_kernel if len(small) == 1 else first_kernel if small[-1].dtype == F32 else last_kernel
    made = [(heads, rows), (heads, rows // 2)] if body is first_kernel else []
    shapes = [jax.ShapeDtypeStruct(s, F32) for s in made] + [jax.ShapeDtypeStruct((n, width), d) for n, d in outs]
    return pl.pallas_call(
        body,
        grid=(1,),
        in_specs=[full(*s.shape) for s in small]
        + [pl.BlockSpec((size, heads * rows), lambda _: (index, 0)), full(*q.shape)],
        out_specs=[full(*s.shape) for s in shapes],
        out_shape=shapes,
        scratch_shapes=[pltpu.VMEM((size, heads * rows), BF16)],
        compiler_params=pltpu.CompilerParams(vmem_limit_bytes=(10 + size // 32) * 2**20),
        cost_estimate=pl.CostEstimate(
            flops=2 * size * heads * rows * width,
            bytes_accessed=4 * size * heads * rows + 2 * q.size,
            transcendentals=0,
        ),
    )(*small, e, q)


def shards(nx, nz, user_states, head_gain, item_table, neg_ids, pos_ids, label_mask, seq_len):
    rows, width = user_states.shape
    heads = head_gain.shape[0]
    table_rows = item_table.shape[0]
    neg_dev = neg_ids.shape[0]
    n_dp = nx * nz * lax.axis_size("core")
    factor = neg_dev * n_dp * lax.axis_size("zh") * lax.axis_size("y") / math.sqrt(rows * n_dp)
    x, z, core = lax.axis_index("x"), lax.axis_index("z"), lax.axis_index("core")
    offset = (lax.axis_index("zh") * lax.axis_size("y") + lax.axis_index("y")) * table_rows

    def shifted(value, axis, size, by):
        return lax.ppermute(value, axis, [(i, (i + by) % size) for i in range(size)])

    other = shifted(user_states, "core", 2, 1)
    table = shifted(item_table, "core", 2, 1)
    gain = shifted(head_gain, "core", 2, 1)
    pos_other = shifted(pos_ids, "core", 2, 1)
    pos_near = shifted(pos_ids, "y", 4, 1)

    slot = lax.broadcasted_iota(jnp.int32, (nx * nz, neg_dev), 0)
    slots = lax.psum(jnp.where(slot == x * nz + z, neg_ids[None], 0), ("x", "z"))

    e, q, m, msg = scores(
        1.0 / math.sqrt(width), nx, nz, x.reshape(1), z.reshape(1), core.reshape(1), offset.reshape(1), slots, pos_near, pos_other,
        gain, user_states, other, table,
    )
    msg = fold(msg, *[lax.ppermute(msg, "y", [(i, i ^ k) for i in range(4)]) for k in (2, 1, 3)])
    part = fold_with_mask(seq_len, label_mask, msg, shifted(msg, "zh", 2, 1))
    cross = shifted(part, "core", 2, 1)

    quarter = nz * neg_dev
    half = quarter // 2
    c, pos_loss, far_a, far_b = grad((part, cross, m), e, q, quarter, 0, [(half, BF16)] * 2)
    far_a, far_b = shifted(far_a, "x", nx, 1), shifted(far_b, "x", nx, -1)
    up_a, up_b, down_a, down_b = grad(
        (c,), e, q, 2 * quarter, 1, [(half, F32), (half, BF16), (half, BF16), (half, F32)]
    )
    up_b, down_a = shifted(up_b, "x", nx, 1), shifted(down_a, "x", nx, -1)
    up_a = shifted((up_a + far_a.astype(F32)).astype(BF16), "x", nx, 1)
    down_b = shifted((down_b + far_b.astype(F32)).astype(BF16), "x", nx, -1)
    own_a, own_b = grad((c, down_a, up_b), e, q, quarter, 1, [(half, F32)] * 2)
    total = jnp.concatenate([own_a + up_a.astype(F32), own_b + down_b.astype(F32)], axis=0)

    parts = {k: total[i * neg_dev : (i + 1) * neg_dev] for i, k in enumerate(Z_ORDER)}
    sent = [shifted(parts[k].astype(BF16), "z", nz, k) for k in Z_ORDER if k]
    out = parts[0]
    for piece in sent:
        out = out + piece.astype(F32)
    return pos_loss, out * factor


def solution(mesh):
    nx, nz = 4, 4
    wide = Mesh(mesh.devices.reshape(nx, nz, 2, 2, 4), DP + TOWER)
    placed = (
        P(DP, None),
        P(),
        P(TOWER, None),
        P(DP + TOWER),
        P(DP),
        P(None, DP),
        P(DP),
    )
    return jax.shard_map(
        functools.partial(shards, nx, nz),
        mesh=wide,
        in_specs=placed,
        out_specs=(P(None, DP), P(DP + TOWER, None)),
        check_vma=False,
    )
```
